32 devices in a mesh: groups: 2 (over x), dp: 8 (over z, y), mp: 2 (over core).
Axes of the slice: x: 2, y: 2, z: 4, core: 2. Of those that a mesh axis runs over, the one named last changes fastest.
Arguments:
- prompt_hidden: bfloat16 [32, 256, 5120], P(('groups', 'dp')), parts along dimension 0, may hold values from -6 to 6
- completion_hidden: bfloat16 [128, 64, 5120], P(('groups', 'dp')), parts along dimension 0, may hold values from -6 to 6
- queries: bfloat16 [128, 64, 4096], P(('groups', 'dp'), None, 'mp'), parts along dimension 0, may hold values from -72 to 72
- cotangent: bfloat16 [128, 64, 4096], P(('groups', 'dp'), None, 'mp'), parts along dimension 0, may hold values from -6 to 6
- kv_weight: bfloat16 [5120, 2, 512], P('dp', None, 'mp'), may hold values from -0.078125 to 0.078125
- prompt_of: int32 [128], P(('groups', 'dp')), parts along dimension 0, may hold values from 0 to 15, as said below
- comp_len: int32 [16, 8], P(('groups', 'dp')), parts along dimension 0, may hold values from 1 to 64, 384 in all within a row
Outputs:
- attended: bfloat16 [128, 64, 4096], P(('groups', 'dp'), None, 'mp'), parts along dimension 0
- grad_queries: bfloat16 [128, 64, 4096], P(('groups', 'dp'), None, 'mp'), parts along dimension 0
- grad_prompt_hidden: bfloat16 [32, 256, 5120], P(('groups', 'dp'), None, 'mp'), parts along dimension 0
- grad_completion_hidden: bfloat16 [128, 64, 5120], P(('groups', 'dp'), None, 'mp'), parts along dimension 0
- grad_kv_weight: float32 [10240, 2, 512], P(('groups', 'dp'), None, 'mp'), parts along dimension 0
The draws below stay inside these ranges and needn't reach their ends.
There are 2 independent parts, one for each index of `groups`. The reference program is written for one: setup_inputs(seed, part) draws one part's arguments, and reference() takes and returns one part's arrays. A program takes and returns all parts, laid end to end along the dimension named above; an argument that names none is the same for every part. Nothing has to cross between parts.
Inputs may be any that keep to these rules, and one draw needn't show every extreme that they name: `prompt_of`: prompt p is held by index p // 2 of dp. The 8 completions held by one index of dp continue prompts of 8 different holders.
All inputs are finite; a program needn't handle non-finite values.
Results may differ from the reference program's by a relative error of at most 0.02.
The reference program's roundings to bfloat16 on the way (of `prompt_kv`, `own_kv`, `weights`, `live_cot`, `score_grad`, `prompt_terms`, `own_grads` and `prompt_grads`) count: a program that leaves them out, or rounds other values in their place, can miss the bound.
Values may be sent and summed in bfloat16 or wider, within the bound.
A program may use at most 192 MiB of HBM per device.

```python
import math
import jax
import jax.numpy as jnp
import numpy as np
from jax import lax

D = 5120
HEADS = 32
KV_HEADS = 4
HEAD_DIM = 128
P_LEN = 256
C_LEN = 64
P_DEV = 2
C_DEV = 8
PROMPTS = 16
COMPS = 64
N_MP = 2


def draw_prompt_of(key, part):
    key = jax.random.fold_in(key, 11)
    row_count = COMPS // C_DEV
    subkeys = jax.random.split(key, row_count + 1)
    shuffles = jax.vmap(lambda single_key: jax.random.permutation(single_key, row_count))(subkeys[:row_count])
    owner_pick = shuffles[:, :C_DEV].astype(jnp.int32)
    slot_pick = jax.random.randint(subkeys[row_count], (row_count, C_DEV), 0, P_DEV).astype(jnp.int32)
    slot_pick = jnp.where(owner_pick == row_count - 1, P_DEV - 1, jnp.where(owner_pick == 0, 0, slot_pick))
    return (owner_pick * P_DEV + slot_pick).reshape(-1).astype(jnp.int32)


def draw_queries(key, part):
    key = jax.random.fold_in(key, 23)
    first_key = jax.random.fold_in(key, 0)
    shape_all = (COMPS, C_LEN, HEADS * HEAD_DIM)
    return (1.5 * jax.random.truncated_normal(first_key, -6.0, 6.0, shape_all, jnp.float32)).astype(jnp.bfloat16)


def levels(rng, dims, shards, low, largest):
    def one(position, shards_of):
        heights = jax.random.uniform(jax.random.fold_in(jax.random.fold_in(rng, 6), position), (shards_of,), jnp.float32, low / len(shards), largest / len(shards))
        return jnp.repeat(jnp.exp(heights), dims[position] // shards_of).reshape((-1,) + (1,) * (len(dims) - position - 1))

    factor_of = one(*shards[0])
    for cut in shards[1:]:
        factor_of = factor_of * one(*cut)
    return factor_of


def split_up(number_of, total, bound, lean):
    loads = [(1 << 20) // math.isqrt(rank ** lean) + 1 for rank in range(2, number_of + 1)]
    rest, holding = total - bound - (number_of - 1), [1] * (number_of - 1)
    while rest > 0:
        candidates = [i for i in range(number_of - 1) if holding[i] < bound]
        mass, left = sum([loads[i] for i in candidates]), rest
        for i in candidates:
            extra = min(bound - holding[i], max(1, left * loads[i] // mass), rest)
            holding[i] = holding[i] + extra
            rest = rest - extra
    return np.array([bound] + holding)


def uneven_parts(stream_key, number_of, total, most, slope):
    if number_of == 2:
        one = jax.random.randint(stream_key, (), max(1, total - most), min(most, total - 1) + 1)
        return jnp.stack([one, total - one])
    sizes = jnp.asarray(split_up(number_of, total, most, slope), jnp.int32)
    couples = (number_of - 1) // 2
    giver, sink = sizes[1:1 + 2 * couples:2], sizes[2:2 + 2 * couples:2]
    margin = jnp.minimum(giver - 1, most - sink)
    shifted = jax.random.randint(jax.random.fold_in(stream_key, 1), (couples,), 0, 1 << 20) % (margin + 1)
    sizes = sizes.at[1:1 + 2 * couples:2].set(giver - shifted).at[2:2 + 2 * couples:2].set(sink + shifted)
    return sizes[jax.random.permutation(jax.random.fold_in(stream_key, 2), number_of)]


def scatter_about(rng, shape, deviation, bound, shards=(), held_as=jnp.bfloat16):
    gain = levels(rng, shape, shards, -0.22, 0.18) if shards else 1.0
    values = jax.random.normal(rng, shape, jnp.float32) * deviation * gain
    return jnp.minimum(jnp.maximum(values, -bound), bound).astype(held_as)


def setup_inputs(seed: int = 0, part: int = 0) -> dict:
    streams_of = jax.random.split(jax.random.key(seed), 8)
    own_keys = jax.random.split(jax.random.fold_in(streams_of[7], part), 8)
    return {
        "prompt_hidden": scatter_about(own_keys[0], (PROMPTS, P_LEN, D), 1.0, 6.0, ((0, 8),)),
        "completion_hidden": scatter_about(own_keys[1], (COMPS, C_LEN, D), 1.0, 6.0, ((0, 8),)),
        "queries": draw_queries(jax.random.fold_in(jax.random.fold_in(streams_of[7], part), 71), part),
        "cotangent": scatter_about(own_keys[3], (COMPS, C_LEN, HEADS * HEAD_DIM), 1.0, 6.0, ((0, 8), (2, 2))),
        "kv_weight": scatter_about(streams_of[4], (D, 2, KV_HEADS * HEAD_DIM), D ** -0.5, 0.078125, ((0, 8), (2, 2))),
        "prompt_of": draw_prompt_of(jax.random.fold_in(jax.random.fold_in(streams_of[7], part), 71), part),
        "comp_len": jax.vmap(lambda own: uneven_parts(own, C_DEV, 3 * C_DEV * C_LEN // 4, C_LEN, 2))(jax.random.split(own_keys[6], (COMPS // C_DEV))).reshape((COMPS // C_DEV, C_DEV)).astype(jnp.int32),
    }


def project(hidden, kv_weight):
    seq_count, seq_len, feat_width = hidden.shape
    flat = jnp.dot(hidden.reshape(seq_count * seq_len, feat_width), kv_weight.reshape(feat_width, -1), preferred_element_type=jnp.float32)
    return flat.astype(jnp.bfloat16).reshape(seq_count, seq_len, 2, -1)


def attend_one(query_rows, prompt_kv, own_kv, length, cotangent):
    group_size = HEADS // KV_HEADS
    score_scale = HEAD_DIM ** -0.5
    key_rows = jnp.concatenate([prompt_kv[:, 0], own_kv[:, 0]], axis=0).astype(jnp.float32).reshape(-1, KV_HEADS, HEAD_DIM)
    value_rows = jnp.concatenate([prompt_kv[:, 1], own_kv[:, 1]], axis=0).astype(jnp.float32).reshape(-1, KV_HEADS, HEAD_DIM)
    query32 = query_rows.astype(jnp.float32).reshape(C_LEN, KV_HEADS, group_size, HEAD_DIM)
    scores = jnp.einsum("ikgd,jkd->kgij", query32, key_rows) * score_scale
    row_ids = jnp.arange(C_LEN, dtype=jnp.int32)[:, None]
    col_ids = jnp.arange(P_LEN + C_LEN, dtype=jnp.int32)[None, :]
    allowed = (col_ids < P_LEN) | (col_ids - P_LEN <= row_ids)
    scores = jnp.where(allowed, scores, -1e30)
    row_max = jnp.max(scores, axis=-1, keepdims=True)
    expo_scores = jnp.exp(scores - row_max)
    probabilities = expo_scores / jnp.sum(expo_scores, axis=-1, keepdims=True)
    weights = probabilities.astype(jnp.bfloat16).astype(jnp.float32)
    live_rows = (jnp.arange(C_LEN, dtype=jnp.int32) < length)[:, None, None, None]
    mixed_out = jnp.einsum("kgij,jkd->ikgd", weights, value_rows)
    mixed_out = jnp.where(live_rows, mixed_out, 0.0)
    attended = mixed_out.reshape(C_LEN, -1).astype(jnp.bfloat16)
    live_cot = jnp.where(live_rows, cotangent.astype(jnp.float32).reshape(C_LEN, KV_HEADS, group_size, HEAD_DIM), 0.0)
    prob_grad = jnp.einsum("ikgd,jkd->kgij", live_cot, value_rows)
    row_delta = jnp.sum(probabilities * prob_grad, axis=-1, keepdims=True)
    score_grad = (probabilities * (prob_grad - row_delta) * score_scale).astype(jnp.bfloat16).astype(jnp.float32)
    grad_queries = jnp.einsum("kgij,jkd->ikgd", score_grad, key_rows).reshape(C_LEN, -1).astype(jnp.bfloat16)
    key_grads = jnp.einsum("kgij,ikgd->jkd", score_grad, query32).reshape(P_LEN + C_LEN, -1)
    value_grads = jnp.einsum("kgij,ikgd->jkd", weights, live_cot).reshape(P_LEN + C_LEN, -1)
    kv_grads = jnp.stack([key_grads, value_grads], axis=1)
    return attended, grad_queries, kv_grads[:P_LEN].astype(jnp.bfloat16), kv_grads[P_LEN:].astype(jnp.bfloat16)


def feature_grads(grads, kv_weight):
    seq_count, seq_len = grads.shape[0], grads.shape[1]
    split_grads = grads.reshape(seq_count * seq_len, 2, N_MP, -1)
    weight_parts = kv_weight.reshape(D, 2, N_MP, -1)
    running = jnp.zeros((seq_count * seq_len, D), jnp.float32)
    for mp_shard in range(N_MP):
        partial_dot = jnp.dot(split_grads[:, :, mp_shard].reshape(seq_count * seq_len, -1), weight_parts[:, :, mp_shard].reshape(D, -1).T, preferred_element_type=jnp.float32)
        running = running + partial_dot.astype(jnp.bfloat16).astype(jnp.float32)
    return running.astype(jnp.bfloat16).reshape(seq_count, seq_len, D)


def reference(prompt_hidden, completion_hidden, queries, cotangent, kv_weight, prompt_of, comp_len):
    prompt_kv = project(prompt_hidden, kv_weight)
    own_kv = project(completion_hidden, kv_weight)
    lengths = comp_len.reshape(-1)

    def single(which):
        return attend_one(queries[which], prompt_kv[prompt_of[which]], own_kv[which], lengths[which], cotangent[which])

    attended, grad_queries, prompt_terms, own_grads = lax.map(single, jnp.arange(COMPS, dtype=jnp.int32))
    summed = jnp.zeros((PROMPTS, P_LEN, 2, KV_HEADS * HEAD_DIM), jnp.float32).at[prompt_of].add(prompt_terms.astype(jnp.float32))
    prompt_grads = summed.astype(jnp.bfloat16)
    grad_prompt_hidden = feature_grads(prompt_grads, kv_weight)
    grad_completion_hidden = feature_grads(own_grads, kv_weight)
    prompt_part = jnp.dot(prompt_hidden.reshape(-1, D).T, prompt_grads.reshape(PROMPTS * P_LEN, -1), preferred_element_type=jnp.float32)
    own_part = jnp.dot(completion_hidden.reshape(-1, D).T, own_grads.reshape(COMPS * C_LEN, -1), preferred_element_type=jnp.float32)
    grad_kv_weight = (prompt_part + own_part).reshape(D, 2, KV_HEADS * HEAD_DIM)
    return attended, grad_queries, grad_prompt_hidden, grad_completion_hidden, grad_kv_weight
```

```python
import functools

import jax
import jax.numpy as jnp
from jax import lax
from jax.experimental import pallas as pl
from jax.experimental.pallas import tpu as pltpu
from jax.sharding import PartitionSpec as P

HEAD_DIM = 128
MESH = pl.DeviceIdType.MESH
F32 = jnp.float32
BF16 = jnp.bfloat16
VMEM_LIMIT = 60 * 1024 * 1024
NT = (((1,), (1,)), ((), ()))
TN = (((0,), (0,)), ((), ()))


def place_of(index, n):
    side = index % 2
    row = index // 2
    return row + side * (n - 1 - 2 * row)


def index_at(place, n):
    place = (place + 2 * n) % n
    back = place // (n // 2)
    return 2 * (place + back * (n - 1 - 2 * place)) + back


def enter(peers):
    barrier = pltpu.get_barrier_semaphore()
    for peer in peers:
        pl.semaphore_signal(barrier, inc=1, device_id=peer, device_id_type=MESH)
    pl.semaphore_wait(barrier, len(peers))


class Ring:
    def __init__(self, buf, send, recv, n):
        self.buf, self.send, self.recv, self.n = buf, send, recv, n
        self.half = buf.shape[1] // 2
        self.place = place_of(lax.axis_index("dp"), n)
        self.copies = []

    def owner(self, way, step):
        return index_at(self.place - step if way == 0 else self.place + step, self.n)

    def pieces(self, way, step):
        if step < self.n // 2 - 1:
            return (0, 1) if way == 0 else (1, 0)
        return (way,)

    def copy(self, way, step, piece):
        to = index_at(self.place + 1 if way == 0 else self.place - 1, self.n)
        block = self.buf.at[self.owner(way, step), pl.ds(piece * self.half, self.half)]
        return pltpu.make_async_remote_copy(
            src_ref=block,
            dst_ref=block,
            send_sem=self.send.at[way, step, piece],
            recv_sem=self.recv.at[way, step, piece],
            device_id={"dp": to},
            device_id_type=MESH,
        )

    def landed(self, way, step, piece):
        block = self.buf.at[self.owner(way, step + 1), pl.ds(piece * self.half, self.half)]
        pltpu.make_async_remote_copy(
            src_ref=block,
            dst_ref=block,
            send_sem=self.send.at[way, step, piece],
            recv_sem=self.recv.at[way, step, piece],
            device_id={"dp": self.owner(1, 1)},
            device_id_type=MESH,
        ).wait_recv()

    def run(self, use):
        last = self.n // 2
        for step in range(last + 1):
            for order in range(2):
                for way in range(2):
                    if step > 0:
                        came = self.pieces(way, step - 1)
                        if order < len(came):
                            self.landed(way, step - 1, came[order])
                    if step < last:
                        going = self.pieces(way, step)
                        if order < len(going):
                            copy = self.copy(way, step, going[order])
                            copy.start()
                            self.copies.append(copy)
            if step == 0 or step == last:
                use([self.owner(0, step)], step)
            else:
                use([self.owner(0, step), self.owner(1, step)], step)

    def finish(self):
        for copy in self.copies:
            copy.wait_send()


def project_kernel(n, w_ref, ph_ref, oh_ref, wall_ref, pkv_ref, own_ref, acc, send_w, recv_w, send_k, recv_k):
    me = lax.axis_index("dp")
    place = place_of(me, n)
    depth = w_ref.shape[0]
    rows = ph_ref.shape[0]
    tile = min(256, rows)
    wall_ref[me] = w_ref[...]
    enter([{"dp": index_at(place + 1, n)}, {"dp": index_at(place - 1, n)}])
    ring = Ring(wall_ref, send_w, recv_w, n)

    def add(owners, step):
        for source, base in ((ph_ref, 0), (oh_ref, rows)):

            @pl.loop(0, rows // tile)
            def _(r):
                at = pl.multiple_of(r * tile, tile)
                total = None
                for owner in owners:
                    cols = pl.ds(pl.multiple_of(owner * depth, 128), depth)
                    term = jnp.dot(source[pl.ds(at, tile), cols], wall_ref[owner], preferred_element_type=F32)
                    total = term if total is None else total + term
                to = pl.ds(base + at, tile)
                if step == 0:
                    acc[to] = total
                else:
                    acc[to] += total

    ring.run(add)
    pkv_ref[me] = acc[:rows].astype(BF16)
    second = Ring(pkv_ref, send_k, recv_k, n)
    second.run(lambda owners, step: None)
    own_ref[...] = acc[rows:].astype(BF16)
    ring.finish()
    second.finish()


def project(w, ph, oh, n):
    depth, width = w.shape
    rows = ph.shape[0]
    sems = pltpu.SemaphoreType.DMA((2, n // 2, 2))
    vmem = pl.BlockSpec(memory_space=pltpu.VMEM)
    return pl.pallas_call(
        functools.partial(project_kernel, n),
        out_shape=(
            jax.ShapeDtypeStruct((n, depth, width), BF16),
            jax.ShapeDtypeStruct((n, rows, width), BF16),
            jax.ShapeDtypeStruct((oh.shape[0], width), BF16),
        ),
        in_specs=[vmem] * 3,
        out_specs=(vmem,) * 3,
        scratch_shapes=[pltpu.VMEM((rows + oh.shape[0], width), F32), sems, sems, sems, sems],
        compiler_params=pltpu.CompilerParams(collective_id=0, has_side_effects=True, vmem_limit_bytes=VMEM_LIMIT),
        name="project_gather",
    )(w, ph, oh)


def attend_kernel(prompt_of, lens, pkv, own, q, cot, att, gq, terms, own_g):
    c = pl.program_id(0)
    length = lens[c]
    slots = own.shape[1]
    width = own.shape[2] // 2
    kv_heads = width // HEAD_DIM
    group = q.shape[2] // HEAD_DIM // kv_heads
    scale = HEAD_DIM ** (-0.5)
    live = lax.broadcasted_iota(jnp.int32, (slots, HEAD_DIM), 0) < length
    cols = group * slots
    key_id = lax.broadcasted_iota(jnp.int32, (slots, cols), 0)
    row_id = lax.broadcasted_iota(jnp.int32, (slots, cols), 1) % slots
    allowed = key_id <= row_id
    for k in range(kv_heads):
        ks = slice(k * HEAD_DIM, (k + 1) * HEAD_DIM)
        vs = slice(width + k * HEAD_DIM, width + (k + 1) * HEAD_DIM)
        kp, ko, vp, vo = pkv[0, :, ks], own[0, :, ks], pkv[0, :, vs], own[0, :, vs]
        heads = [slice((k * group + g) * HEAD_DIM, (k * group + g + 1) * HEAD_DIM) for g in range(group)]
        qk = jnp.concatenate([q[0, :, h] for h in heads], axis=0)
        do = jnp.concatenate(
            [jnp.where(live, cot[0, :, h].astype(F32), 0.0).astype(BF16) for h in heads], axis=0
        )
        sp = lax.dot_general(kp, qk, NT, preferred_element_type=F32)
        so = lax.dot_general(ko, qk, NT, preferred_element_type=F32)
        so = jnp.where(allowed, so, -1e30)
        top = jnp.maximum(jnp.max(sp, axis=0, keepdims=True), jnp.max(so, axis=0, keepdims=True))
        ep = jnp.exp((sp - top) * scale)
        eo = jnp.exp((so - top) * scale)
        inv = 1.0 / (jnp.sum(ep, axis=0, keepdims=True) + jnp.sum(eo, axis=0, keepdims=True))
        pp = ep * inv
        po = eo * inv
        wp = pp.astype(BF16)
        wo = po.astype(BF16)
        dp = lax.dot_general(vp, do, NT, preferred_element_type=F32)
        dn = lax.dot_general(vo, do, NT, preferred_element_type=F32)
        delta = jnp.sum(pp * dp, axis=0, keepdims=True) + jnp.sum(po * dn, axis=0, keepdims=True)
        gp = (pp * (dp - delta) * scale).astype(BF16)
        go = (po * (dn - delta) * scale).astype(BF16)
        mixed = lax.dot_general(vp, wp, TN, preferred_element_type=F32) + lax.dot_general(
            vo, wo, TN, preferred_element_type=F32
        )
        dq = lax.dot_general(kp, gp, TN, preferred_element_type=F32) + lax.dot_general(
            ko, go, TN, preferred_element_type=F32
        )
        mixed = mixed.T
        dq = dq.T
        for g, h in enumerate(heads):
            rows = slice(g * slots, (g + 1) * slots)
            att[0, :, h] = jnp.where(live, mixed[rows], 0.0).astype(BF16)
            gq[0, :, h] = dq[rows].astype(BF16)
        terms[0, :, ks] = jnp.dot(gp, qk, preferred_element_type=F32).astype(BF16)
        terms[0, :, vs] = jnp.dot(wp, do, preferred_element_type=F32).astype(BF16)
        own_g[0, :, ks] = jnp.dot(go, qk, preferred_element_type=F32).astype(BF16)
        own_g[0, :, vs] = jnp.dot(wo, do, preferred_element_type=F32).astype(BF16)


def attend(prompt_of, lens, pkv, own, q, cot, n):
    comps, slots, features = q.shape
    prompts, plen, width = pkv.shape
    per = prompts // n
    one = lambda c, p, l: (c, 0, 0)
    wide = pl.BlockSpec((1, slots, features), one)
    thin = pl.BlockSpec((1, slots, width), one)
    return pl.pallas_call(
        attend_kernel,
        out_shape=(
            jax.ShapeDtypeStruct(q.shape, BF16),
            jax.ShapeDtypeStruct(q.shape, BF16),
            jax.ShapeDtypeStruct((n, plen, width), BF16),
            jax.ShapeDtypeStruct((comps, slots, width), BF16),
        ),
        grid_spec=pltpu.PrefetchScalarGridSpec(
            num_scalar_prefetch=2,
            grid=(comps,),
            in_specs=[pl.BlockSpec((1, plen, width), lambda c, p, l: (p[c], 0, 0)), thin, wide, wide],
            out_specs=(wide, wide, pl.BlockSpec((1, plen, width), lambda c, p, l: (p[c] // per, 0, 0)), thin),
        ),
        compiler_params=pltpu.CompilerParams(vmem_limit_bytes=VMEM_LIMIT),
        name="attend",
    )(prompt_of, lens, pkv, own, q, cot)


def swap_kernel(n, src, dst, send, recv, here):
    me = lax.axis_index("dp")
    place = place_of(me, n)
    peers = [index_at(place + d, n) for d in range(1, n)]
    own = pltpu.make_async_copy(src.at[me], dst.at[me], here)
    own.start()
    enter([{"dp": peer} for peer in peers])
    order = sorted(range(1, n), key=lambda d: -min(d, n - d))
    copies = []
    for d in order:
        peer = peers[d - 1]
        copy = pltpu.make_async_remote_copy(
            src_ref=src.at[peer],
            dst_ref=dst.at[me],
            send_sem=send.at[d],
            recv_sem=recv.at[d],
            device_id={"dp": peer},
            device_id_type=MESH,
        )
        copy.start()
        copies.append(copy)
    own.wait()
    for d in order:
        came = index_at(place - d, n)
        pltpu.make_async_remote_copy(
            src_ref=dst.at[came],
            dst_ref=dst.at[came],
            send_sem=send.at[d],
            recv_sem=recv.at[d],
            device_id={"dp": peers[0]},
            device_id_type=MESH,
        ).wait_recv()
    for copy in copies:
        copy.wait_send()


def swap(terms, n):
    vmem = pl.BlockSpec(memory_space=pltpu.VMEM)
    return pl.pallas_call(
        functools.partial(swap_kernel, n),
        out_shape=jax.ShapeDtypeStruct(terms.shape, terms.dtype),
        in_specs=[vmem],
        out_specs=vmem,
        scratch_shapes=[
            pltpu.SemaphoreType.DMA((n,)),
            pltpu.SemaphoreType.DMA((n,)),
            pltpu.SemaphoreType.DMA,
        ],
        compiler_params=pltpu.CompilerParams(collective_id=1, has_side_effects=True, vmem_limit_bytes=VMEM_LIMIT),
        name="swap_terms",
    )(terms)


def grads_kernel(
    n, chunk, g_ref, gt_ref, ph_ref, oh_ref, wall_ref, fp_ref, fo_ref, gw_ref,
    slots, fsend, frecv, send, recv, send_f, recv_f,
):
    me = lax.axis_index("dp")
    mp = lax.axis_index("mp")
    place = place_of(me, n)
    right = index_at(place + 1, n)
    left = index_at(place - 1, n)
    other = {"mp": 1 - mp}
    rows = ph_ref.shape[0]
    depth = gw_ref.shape[0]
    half = gt_ref.shape[0] // 2
    last = n // 2
    chunks = fsend.shape[0]
    tile = min(256, rows)
    enter([{"dp": right}, {"dp": left}, other])

    def partial(target, piece):
        cols = pl.ds(pl.multiple_of(target * depth, 128), depth)
        top = gt_ref[piece * half : (piece + 1) * half]
        return jnp.dot(top[:, :rows], ph_ref[:, cols], preferred_element_type=F32) + jnp.dot(
            top[:, rows:], oh_ref[:, cols], preferred_element_type=F32
        )

    def copy(way, step, piece):
        return pltpu.make_async_remote_copy(
            src_ref=slots.at[way, step, piece],
            dst_ref=slots.at[way, step + 1, piece],
            send_sem=send.at[way, step, piece],
            recv_sem=recv.at[way, step, piece],
            device_id={"dp": right if way == 0 else left},
            device_id_type=MESH,
        )

    started = []

    def go(way, step, piece):
        one = copy(way, step, piece)
        one.start()
        started.append(one)

    far = index_at(place + last, n)
    for way in range(2):
        slots[way, 0, way] = partial(far, way)
        go(way, 0, way)
    for way in range(2):
        near = index_at(place + (last - 1) if way == 0 else place - (last - 1), n)
        slots[way, 1, 1 - way] = partial(near, 1 - way)
        go(way, 1, 1 - way)

    def product(first, at):
        return lax.dot_general(
            g_ref[pl.ds(at, tile)], wall_ref[pl.ds(first, chunk)], NT, preferred_element_type=F32
        ).astype(BF16)

    feature = []
    span = chunk * chunks
    for j in range(chunks):
        first = pl.multiple_of((1 - mp) * span + j * chunk, 128)

        @pl.loop(0, 2 * rows // tile)
        def _(r):
            at = pl.multiple_of(r * tile, tile)
            fsend[j, pl.ds(at, tile)] = product(first, at)

        one = pltpu.make_async_remote_copy(
            src_ref=fsend.at[j],
            dst_ref=frecv.at[j],
            send_sem=send_f.at[j],
            recv_sem=recv_f.at[j],
            device_id=other,
            device_id_type=MESH,
        )
        one.start()
        feature.append(one)
    for j in range(chunks):
        first = pl.multiple_of(mp * span + j * chunk, 128)
        feature[j].wait_recv()

        @pl.loop(0, rows // tile)
        def _(r):
            at = pl.multiple_of(r * tile, tile)
            cols = slice(j * chunk, (j + 1) * chunk)
            got = frecv[j, pl.ds(at, tile)].astype(F32)
            fp_ref[pl.ds(at, tile), cols] = (product(first, at).astype(F32) + got).astype(BF16)
            low = pl.multiple_of(rows + at, tile)
            got = frecv[j, pl.ds(low, tile)].astype(F32)
            fo_ref[pl.ds(at, tile), cols] = (product(first, low).astype(F32) + got).astype(BF16)

    for step in range(1, last):
        for order in range(2):
            for way in range(2):
                piece = way if order == 0 else 1 - way
                if step == 1 and piece != way:
                    continue
                target = index_at(place + (last - step) if way == 0 else place - (last - step), n)
                copy(way, step - 1, piece).wait_recv()
                slots[way, step, piece] += partial(target, piece)
                go(way, step, piece)
    for piece in range(2):
        mine = partial(me, piece)
        for way in range(2):
            copy(way, last - 1, piece).wait_recv()
        total = mine + slots[0, last, piece] + slots[1, last, piece]
        gw_ref[:, piece * half : (piece + 1) * half] = total.T
    for one in started:
        one.wait_send()
    for one in feature:
        one.wait_send()


def grads(g, ph, oh, wall, n, n_mp):
    rows, model_dim = ph.shape
    width = g.shape[1]
    depth = model_dim // n
    share = model_dim // n_mp
    chunk = 512 if share % 512 == 0 else 128
    chunks = share // chunk
    vmem = pl.BlockSpec(memory_space=pltpu.VMEM)
    sems = pltpu.SemaphoreType.DMA((2, n // 2, 2))
    return pl.pallas_call(
        functools.partial(grads_kernel, n, chunk),
        out_shape=(
            jax.ShapeDtypeStruct((rows, share), BF16),
            jax.ShapeDtypeStruct((rows, share), BF16),
            jax.ShapeDtypeStruct((depth, width), F32),
        ),
        in_specs=[vmem] * 5,
        out_specs=(vmem,) * 3,
        scratch_shapes=[
            pltpu.VMEM((2, n // 2 + 1, 2, width // 2, depth), F32),
            pltpu.VMEM((chunks, 2 * rows, chunk), BF16),
            pltpu.VMEM((chunks, 2 * rows, chunk), BF16),
            sems,
            sems,
            pltpu.SemaphoreType.DMA((chunks,)),
            pltpu.SemaphoreType.DMA((chunks,)),
        ],
        compiler_params=pltpu.CompilerParams(collective_id=2, has_side_effects=True, vmem_limit_bytes=VMEM_LIMIT),
        name="grads_reduce",
    )(g, g.T, ph, oh, wall)


def shards(n, n_mp, prompt_hidden, completion_hidden, queries, cotangent, kv_weight, prompt_of, comp_len):
    per, plen, model_dim = prompt_hidden.shape
    comps, slots, _ = completion_hidden.shape
    depth, _, kv_width = kv_weight.shape
    width = 2 * kv_width
    w = kv_weight.reshape(depth, width)
    ph = prompt_hidden.reshape(per * plen, model_dim)
    oh = completion_hidden.reshape(comps * slots, model_dim)
    wall, pkv, own = project(w, ph, oh, n)
    pkv = pkv.reshape(n * per, plen, width)
    attended, grad_queries, terms, own_grads = attend(
        prompt_of, comp_len.reshape(-1), pkv, own.reshape(comps, slots, width), queries, cotangent, n
    )
    got = swap(terms, n)
    everyone = lax.all_gather(prompt_of, "dp", axis=0, tiled=False)
    mine = lax.axis_index("dp") * per + jnp.arange(per, dtype=jnp.int32)
    hit = jnp.any(everyone[:, :, None] == mine[None, None, :], axis=1)
    prompt_grads = jnp.stack(
        [jnp.sum(jnp.where(hit[:, s, None, None], got.astype(F32), 0.0), axis=0) for s in range(per)]
    ).astype(BF16)
    g = jnp.concatenate([prompt_grads.reshape(per * plen, width), own_grads.reshape(comps * slots, width)], axis=0)
    fp, fo, gw = grads(g, ph, oh, wall.reshape(model_dim, width), n, n_mp)
    return (
        attended,
        grad_queries,
        fp.reshape(per, plen, -1),
        fo.reshape(comps, slots, -1),
        gw.reshape(depth, 2, kv_width),
    )


def solution(mesh):
    in_specs = (
        P(("groups", "dp"), None, None),
        P(("groups", "dp"), None, None),
        P(("groups", "dp"), None, "mp"),
        P(("groups", "dp"), None, "mp"),
        P("dp", None, "mp"),
        P(("groups", "dp")),
        P(("groups", "dp"), None),
    )
    out_specs = (P(("groups", "dp"), None, "mp"),) * 5
    body = functools.partial(shards, mesh.shape["dp"], mesh.shape["mp"])
    return jax.shard_map(body, mesh=mesh, in_specs=in_specs, out_specs=out_specs, check_vma=False)
```

```python
import functools

import jax
import jax.numpy as jnp
from jax import lax
from jax.experimental import pallas as pl
from jax.experimental.pallas import tpu as pltpu
from jax.sharding import PartitionSpec as P

HEAD_DIM = 128
MESH = pl.DeviceIdType.MESH
F32 = jnp.float32
BF16 = jnp.bfloat16
VMEM_LIMIT = 60 * 1024 * 1024
NT = (((1,), (1,)), ((), ()))
TN = (((0,), (0,)), ((), ()))
EXTRA = 16
STEPS = 32000.0


def place_of(index, n):
    side = index % 2
    row = index // 2
    return row + side * (n - 1 - 2 * row)


def index_at(place, n):
    place = (place + 2 * n) % n
    back = place // (n // 2)
    return 2 * (place + back * (n - 1 - 2 * place)) + back


def enter(peers):
    barrier = pltpu.get_barrier_semaphore()
    for peer in peers:
        pl.semaphore_signal(barrier, inc=1, device_id=peer, device_id_type=MESH)
    pl.semaphore_wait(barrier, len(peers))


class Ring:
    def __init__(self, buf, send, recv, n):
        self.buf, self.send, self.recv, self.n = buf, send, recv, n
        self.half = buf.shape[1] // 2
        self.place = place_of(lax.axis_index("dp"), n)
        self.copies = []

    def owner(self, way, step):
        return index_at(self.place - step if way == 0 else self.place + step, self.n)

    def pieces(self, way, step):
        if step < self.n // 2 - 1:
            return (0, 1) if way == 0 else (1, 0)
        return (way,)

    def copy(self, way, step, piece):
        to = index_at(self.place + 1 if way == 0 else self.place - 1, self.n)
        block = self.buf.at[self.owner(way, step), pl.ds(piece * self.half, self.half)]
        return pltpu.make_async_remote_copy(
            src_ref=block,
            dst_ref=block,
            send_sem=self.send.at[way, step, piece],
            recv_sem=self.recv.at[way, step, piece],
            device_id={"dp": to},
            device_id_type=MESH,
        )

    def landed(self, way, step, piece):
        block = self.buf.at[self.owner(way, step + 1), pl.ds(piece * self.half, self.half)]
        pltpu.make_async_remote_copy(
            src_ref=block,
            dst_ref=block,
            send_sem=self.send.at[way, step, piece],
            recv_sem=self.recv.at[way, step, piece],
            device_id={"dp": self.owner(1, 1)},
            device_id_type=MESH,
        ).wait_recv()

    def run(self, use):
        last = self.n // 2
        for step in range(last + 1):
            for order in range(2):
                for way in range(2):
                    if step > 0:
                        came = self.pieces(way, step - 1)
                        if order < len(came):
                            self.landed(way, step - 1, came[order])
                    if step < last:
                        going = self.pieces(way, step)
                        if order < len(going):
                            copy = self.copy(way, step, going[order])
                            copy.start()
                            self.copies.append(copy)
            if step == 0 or step == last:
                use([self.owner(0, step)], step)
            else:
                use([self.owner(0, step), self.owner(1, step)], step)

    def finish(self):
        for copy in self.copies:
            copy.wait_send()


def project_kernel(
    n, w_ref, ph_hbm, oh_hbm, wall_ref, pkv_ref, own_ref, ph_ref, oh_ref, acc, load, send_w, recv_w, send_k, recv_k
):
    me = lax.axis_index("dp")
    place = place_of(me, n)
    depth = w_ref.shape[0]
    rows = ph_ref.shape[0]
    tile = min(256, rows)
    loads = [
        pltpu.make_async_copy(src, dst, load.at[i])
        for i, (src, dst) in enumerate(((ph_hbm, ph_ref), (oh_hbm, oh_ref)))
    ]
    for one in loads:
        one.start()
    wall_ref[me] = w_ref[...]
    enter([{"dp": index_at(place + 1, n)}, {"dp": index_at(place - 1, n)}])
    ring = Ring(wall_ref, send_w, recv_w, n)

    def add(owners, step):
        if step == 0:
            for one in loads:
                one.wait()
        for source, base in ((ph_ref, 0), (oh_ref, rows)):

            @pl.loop(0, rows // tile)
            def _(r):
                at = pl.multiple_of(r * tile, tile)
                total = None
                for owner in owners:
                    cols = pl.ds(pl.multiple_of(owner * depth, 128), depth)
                    term = jnp.dot(source[pl.ds(at, tile), cols], wall_ref[owner], preferred_element_type=F32)
                    total = term if total is None else total + term
                to = pl.ds(base + at, tile)
                if step == 0:
                    acc[to] = total
                else:
                    acc[to] += total

    ring.run(add)
    pkv_ref[me] = acc[:rows].astype(BF16)
    second = Ring(pkv_ref, send_k, recv_k, n)
    second.run(lambda owners, step: None)
    own_ref[...] = acc[rows:].astype(BF16)
    ring.finish()
    second.finish()


def project(w, ph, oh, n):
    depth, width = w.shape
    rows = ph.shape[0]
    sems = pltpu.SemaphoreType.DMA((2, n // 2, 2))
    vmem = pl.BlockSpec(memory_space=pltpu.VMEM)
    return pl.pallas_call(
        functools.partial(project_kernel, n),
        out_shape=(
            jax.ShapeDtypeStruct((n, depth, width), BF16),
            jax.ShapeDtypeStruct((n, rows, width), BF16),
            jax.ShapeDtypeStruct((oh.shape[0], width), BF16),
        ),
        in_specs=[vmem] + [pl.BlockSpec(memory_space=pl.ANY)] * 2,
        out_specs=(vmem,) * 3,
        scratch_shapes=[
            pltpu.VMEM(ph.shape, BF16),
            pltpu.VMEM(oh.shape, BF16),
            pltpu.VMEM((rows + oh.shape[0], width), F32),
            pltpu.SemaphoreType.DMA((2,)),
            sems,
            sems,
            sems,
            sems,
        ],
        compiler_params=pltpu.CompilerParams(collective_id=0, has_side_effects=True, vmem_limit_bytes=VMEM_LIMIT),
        name="project_gather",
    )(w, ph, oh)


def attend_kernel(per, prompt_of, lens, pkv, own, q, cot, *rest):
    att, gq, terms, own_g = rest[-4:]
    c = pl.program_id(0)
    plen = pkv.shape[1]
    length = lens[c]
    slots = own.shape[1]
    width = own.shape[2] // 2
    kv_heads = width // HEAD_DIM
    group = q.shape[2] // HEAD_DIM // kv_heads
    scale = HEAD_DIM ** (-0.5)
    live = lax.broadcasted_iota(jnp.int32, (slots, HEAD_DIM), 0) < length
    cols = group * slots
    key_id = lax.broadcasted_iota(jnp.int32, (slots, cols), 0)
    row_id = lax.broadcasted_iota(jnp.int32, (slots, cols), 1) % slots
    allowed = key_id <= row_id
    mark = (prompt_of[c] % per + 1).astype(F32)
    terms[0, plen:] = jnp.full((EXTRA, 2 * width), mark, F32).astype(BF16)
    for k in range(kv_heads):
        ks = slice(k * HEAD_DIM, (k + 1) * HEAD_DIM)
        vs = slice(width + k * HEAD_DIM, width + (k + 1) * HEAD_DIM)
        kp, ko, vp, vo = pkv[0, :, ks], own[0, :, ks], pkv[0, :, vs], own[0, :, vs]
        heads = [slice((k * group + g) * HEAD_DIM, (k * group + g + 1) * HEAD_DIM) for g in range(group)]
        qk = jnp.concatenate([q[0, :, h] for h in heads], axis=0)
        do = jnp.concatenate(
            [jnp.where(live, cot[0, :, h].astype(F32), 0.0).astype(BF16) for h in heads], axis=0
        )
        sp = lax.dot_general(kp, qk, NT, preferred_element_type=F32)
        so = lax.dot_general(ko, qk, NT, preferred_element_type=F32)
        so = jnp.where(allowed, so, -1e30)
        top = jnp.maximum(jnp.max(sp, axis=0, keepdims=True), jnp.max(so, axis=0, keepdims=True))
        ep = jnp.exp((sp - top) * scale)
        eo = jnp.exp((so - top) * scale)
        inv = 1.0 / (jnp.sum(ep, axis=0, keepdims=True) + jnp.sum(eo, axis=0, keepdims=True))
        pp = ep * inv
        po = eo * inv
        wp = pp.astype(BF16)
        wo = po.astype(BF16)
        dp = lax.dot_general(vp, do, NT, preferred_element_type=F32)
        dn = lax.dot_general(vo, do, NT, preferred_element_type=F32)
        delta = jnp.sum(pp * dp, axis=0, keepdims=True) + jnp.sum(po * dn, axis=0, keepdims=True)
        gp = (pp * (dp - delta) * scale).astype(BF16)
        go = (po * (dn - delta) * scale).astype(BF16)
        mixed = lax.dot_general(vp, wp, TN, preferred_element_type=F32) + lax.dot_general(
            vo, wo, TN, preferred_element_type=F32
        )
        dq = lax.dot_general(kp, gp, TN, preferred_element_type=F32) + lax.dot_general(
            ko, go, TN, preferred_element_type=F32
        )
        mixed = mixed.T
        dq = dq.T
        for g, h in enumerate(heads):
            rows = slice(g * slots, (g + 1) * slots)
            att[0, :, h] = jnp.where(live, mixed[rows], 0.0).astype(BF16)
            gq[0, :, h] = dq[rows].astype(BF16)
        terms[0, :plen, ks] = jnp.dot(gp, qk, preferred_element_type=F32).astype(BF16)
        terms[0, :plen, vs] = jnp.dot(wp, do, preferred_element_type=F32).astype(BF16)
        own_g[0, :, ks] = jnp.dot(go, qk, preferred_element_type=F32).astype(BF16)
        own_g[0, :, vs] = jnp.dot(wo, do, preferred_element_type=F32).astype(BF16)


def attend(prompt_of, lens, pkv, own, q, cot, n):
    comps, slots, features = q.shape
    prompts, plen, width = pkv.shape
    per = prompts // n
    one = lambda c, p, l: (c, 0, 0)
    wide = pl.BlockSpec((1, slots, features), one)
    thin = pl.BlockSpec((1, slots, width), one)
    held = (n, plen + EXTRA, width)
    blank = [] if n <= comps else [jnp.zeros(held, BF16)]
    return pl.pallas_call(
        functools.partial(attend_kernel, per),
        out_shape=(
            jax.ShapeDtypeStruct(q.shape, BF16),
            jax.ShapeDtypeStruct(q.shape, BF16),
            jax.ShapeDtypeStruct(held, BF16),
            jax.ShapeDtypeStruct((comps, slots, width), BF16),
        ),
        grid_spec=pltpu.PrefetchScalarGridSpec(
            num_scalar_prefetch=2,
            grid=(comps,),
            in_specs=[pl.BlockSpec((1, plen, width), lambda c, p, l: (p[c], 0, 0)), thin, wide, wide]
            + [pl.BlockSpec(memory_space=pl.ANY)] * len(blank),
            out_specs=(wide, wide, pl.BlockSpec((1, plen + EXTRA, width), lambda c, p, l: (p[c] // per, 0, 0)), thin),
        ),
        input_output_aliases={6: 2} if blank else {},
        compiler_params=pltpu.CompilerParams(vmem_limit_bytes=VMEM_LIMIT),
        name="attend",
    )(prompt_of, lens, pkv, own, q, cot, *blank)


def encode(block, ref):
    top = jnp.maximum(jnp.max(jnp.abs(block), axis=0, keepdims=True), 1e-30)
    power = jnp.ceil(jnp.log2(top))
    rows = block.shape[0]
    ref[:rows] = jnp.round(block * (jnp.exp2(-power) * STEPS)).astype(jnp.int32).astype(jnp.int16)
    ref[rows:] = jnp.broadcast_to(power, (EXTRA, block.shape[1])).astype(jnp.int32).astype(jnp.int16)


def decode(ref):
    rows = ref.shape[0] - EXTRA
    power = ref[rows:].astype(jnp.int32).astype(F32)[:1]
    return ref[:rows].astype(jnp.int32).astype(F32) * (jnp.exp2(power) * (1.0 / STEPS))


def grads_kernel(
    n, chunk, per, terms_ref, own_ref, ph_hbm, oh_hbm, wall_hbm, fp_ref, fo_ref, gw_ref,
    got, g_ref, gt_ref, ph_ref, oh_ref, wall_ref, slots, fsend, frecv,
    load, here, send_t, recv_t, send, recv, send_f, recv_f,
):
    me = lax.axis_index("dp")
    mp = lax.axis_index("mp")
    place = place_of(me, n)
    right = index_at(place + 1, n)
    left = index_at(place - 1, n)
    other = {"mp": 1 - mp}
    rows = ph_ref.shape[0]
    plen = rows // per
    depth = gw_ref.shape[0]
    width = gt_ref.shape[0]
    half = width // 2
    last = n // 2
    chunks = fsend.shape[1]
    tile = min(256, rows)
    loads = [
        pltpu.make_async_copy(src, dst, load.at[i])
        for i, (src, dst) in enumerate(((wall_hbm, wall_ref), (oh_hbm, oh_ref), (ph_hbm, ph_ref)))
    ]
    own_copy = pltpu.make_async_copy(terms_ref.at[me], got.at[me], here)
    own_copy.start()
    for one in loads:
        one.start()
    peers = [index_at(place + d, n) for d in range(1, n)]
    enter([{"dp": peer} for peer in peers] + [other])
    order = sorted(range(1, n), key=lambda d: -min(d, n - d))
    swaps = []
    for d in order:
        peer = peers[d - 1]
        one = pltpu.make_async_remote_copy(
            src_ref=terms_ref.at[peer],
            dst_ref=got.at[me],
            send_sem=send_t.at[d],
            recv_sem=recv_t.at[d],
            device_id={"dp": peer},
            device_id_type=MESH,
        )
        one.start()
        swaps.append(one)
    span = chunk * chunks

    def product(first, at):
        return lax.dot_general(
            g_ref[pl.ds(at, tile)], wall_ref[pl.ds(first, chunk)], NT, preferred_element_type=F32
        ).astype(BF16)

    feature = {}

    def away(part):
        for j in range(chunks):
            first = pl.multiple_of((1 - mp) * span + j * chunk, 128)

            @pl.loop(0, rows // tile)
            def _(r):
                at = pl.multiple_of(r * tile, tile)
                fsend[part, j, pl.ds(at, tile)] = product(first, pl.multiple_of(part * rows + at, tile))

            one = pltpu.make_async_remote_copy(
                src_ref=fsend.at[part, j],
                dst_ref=frecv.at[part, j],
                send_sem=send_f.at[part, j],
                recv_sem=recv_f.at[part, j],
                device_id=other,
                device_id_type=MESH,
            )
            one.start()
            feature[part, j] = one

    def home(part, out_ref):
        for j in range(chunks):
            first = pl.multiple_of(mp * span + j * chunk, 128)
            feature[part, j].wait_recv()

            @pl.loop(0, rows // tile)
            def _(r):
                at = pl.multiple_of(r * tile, tile)
                mine = product(first, pl.multiple_of(part * rows + at, tile)).astype(F32)
                total = mine + frecv[part, j, pl.ds(at, tile)].astype(F32)
                out_ref[pl.ds(at, tile), j * chunk : (j + 1) * chunk] = total.astype(BF16)

    g_ref[rows:] = own_ref[...]
    gt_ref[:, rows:] = own_ref[...].astype(F32).T.astype(BF16)
    loads[0].wait()
    away(1)
    home(1, fo_ref)
    loads[1].wait()
    loads[2].wait()
    own_copy.wait()
    for d in order:
        came = index_at(place - d, n)
        pltpu.make_async_remote_copy(
            src_ref=got.at[came],
            dst_ref=got.at[came],
            send_sem=send_t.at[d],
            recv_sem=recv_t.at[d],
            device_id={"dp": peers[0]},
            device_id_type=MESH,
        ).wait_recv()
    for s in range(per):
        for lane in range(0, width, half):
            cols = slice(lane, lane + half)
            total = jnp.zeros((plen, half), F32)
            for e in range(n):
                mark = got[e, plen:, cols].astype(F32)[:1]
                total = total + jnp.where(mark == float(s + 1), got[e, :plen, cols].astype(F32), 0.0)
            kept = total.astype(BF16)
            g_ref[s * plen : (s + 1) * plen, cols] = kept
            gt_ref[cols, s * plen : (s + 1) * plen] = kept.astype(F32).T.astype(BF16)

    def partial(target, piece):
        cols = pl.ds(pl.multiple_of(target * depth, 128), depth)
        top = gt_ref[piece * half : (piece + 1) * half]
        return jnp.dot(top[:, :rows], ph_ref[:, cols], preferred_element_type=F32) + jnp.dot(
            top[:, rows:], oh_ref[:, cols], preferred_element_type=F32
        )

    def copy(way, step, piece):
        return pltpu.make_async_remote_copy(
            src_ref=slots.at[way, step, piece],
            dst_ref=slots.at[way, step + 1, piece],
            send_sem=send.at[way, step, piece],
            recv_sem=recv.at[way, step, piece],
            device_id={"dp": right if way == 0 else left},
            device_id_type=MESH,
        )

    started = []

    def go(way, step, piece):
        one = copy(way, step, piece)
        one.start()
        started.append(one)

    far = index_at(place + last, n)
    for way in range(2):
        encode(partial(far, way), slots.at[way, 0, way])
        go(way, 0, way)
    for way in range(2):
        near = index_at(place + (last - 1) if way == 0 else place - (last - 1), n)
        encode(partial(near, 1 - way), slots.at[way, 1, 1 - way])
        go(way, 1, 1 - way)
    away(0)
    for step in range(1, last):
        for turn in range(2):
            for way in range(2):
                piece = way if turn == 0 else 1 - way
                if step == 1 and piece != way:
                    continue
                target = index_at(place + (last - step) if way == 0 else place - (last - step), n)
                mine = partial(target, piece)
                copy(way, step - 1, piece).wait_recv()
                encode(decode(slots.at[way, step, piece]) + mine, slots.at[way, step, piece])
                go(way, step, piece)
        if step == 1:
            home(0, fp_ref)
    for piece in range(2):
        mine = partial(me, piece)
        for way in range(2):
            copy(way, last - 1, piece).wait_recv()
        total = mine + decode(slots.at[0, last, piece]) + decode(slots.at[1, last, piece])
        gw_ref[:, piece * half : (piece + 1) * half] = total.T
    for one in started + swaps + list(feature.values()):
        one.wait_send()


def grads(terms, own_g, ph, oh, wall, n, n_mp, per):
    rows, model_dim = ph.shape
    width = own_g.shape[1]
    depth = model_dim // n
    share = model_dim // n_mp
    chunk = 512 if share % 512 == 0 else 128
    chunks = share // chunk
    vmem = pl.BlockSpec(memory_space=pltpu.VMEM)
    hbm = pl.BlockSpec(memory_space=pl.ANY)
    sems = pltpu.SemaphoreType.DMA((2, n // 2, 2))
    return pl.pallas_call(
        functools.partial(grads_kernel, n, chunk, per),
        out_shape=(
            jax.ShapeDtypeStruct((rows, share), BF16),
            jax.ShapeDtypeStruct((rows, share), BF16),
            jax.ShapeDtypeStruct((depth, width), F32),
        ),
        in_specs=[vmem, vmem, hbm, hbm, hbm],
        out_specs=(vmem,) * 3,
        scratch_shapes=[
            pltpu.VMEM(terms.shape, BF16),
            pltpu.VMEM((2 * rows, width), BF16),
            pltpu.VMEM((width, 2 * rows), BF16),
            pltpu.VMEM(ph.shape, BF16),
            pltpu.VMEM(oh.shape, BF16),
            pltpu.VMEM(wall.shape, BF16),
            pltpu.VMEM((2, n // 2 + 1, 2, width // 2 + EXTRA, depth), jnp.int16),
            pltpu.VMEM((2, chunks, rows, chunk), BF16),
            pltpu.VMEM((2, chunks, rows, chunk), BF16),
            pltpu.SemaphoreType.DMA((3,)),
            pltpu.SemaphoreType.DMA,
            pltpu.SemaphoreType.DMA((n,)),
            pltpu.SemaphoreType.DMA((n,)),
            sems,
            sems,
            pltpu.SemaphoreType.DMA((2, chunks)),
            pltpu.SemaphoreType.DMA((2, chunks)),
        ],
        compiler_params=pltpu.CompilerParams(collective_id=2, has_side_effects=True, vmem_limit_bytes=VMEM_LIMIT),
        name="grads_reduce",
    )(terms, own_g, ph, oh, wall)


def shards(n, n_mp, prompt_hidden, completion_hidden, queries, cotangent, kv_weight, prompt_of, comp_len):
    per, plen, model_dim = prompt_hidden.shape
    comps, slots, _ = completion_hidden.shape
    depth, _, kv_width = kv_weight.shape
    width = 2 * kv_width
    w = kv_weight.reshape(depth, width)
    ph = prompt_hidden.reshape(per * plen, model_dim)
    oh = completion_hidden.reshape(comps * slots, model_dim)
    wall, pkv, own = project(w, ph, oh, n)
    pkv = pkv.reshape(n * per, plen, width)
    attended, grad_queries, terms, own_grads = attend(
        prompt_of, comp_len.reshape(-1), pkv, own.reshape(comps, slots, width), queries, cotangent, n
    )
    fp, fo, gw = grads(
        terms, own_grads.reshape(comps * slots, width), ph, oh, wall.reshape(model_dim, width), n, n_mp, per
    )
    return (
        attended,
        grad_queries,
        fp.reshape(per, plen, -1),
        fo.reshape(comps, slots, -1),
        gw.reshape(depth, 2, kv_width),
    )


def solution(mesh):
    in_specs = (
        P(("groups", "dp"), None, None),
        P(("groups", "dp"), None, None),
        P(("groups", "dp"), None, "mp"),
        P(("groups", "dp"), None, "mp"),
        P("dp", None, "mp"),
        P(("groups", "dp")),
        P(("groups", "dp"), None),
    )
    out_specs = (P(("groups", "dp"), None, "mp"),) * 5
    body = functools.partial(shards, mesh.shape["dp"], mesh.shape["mp"])
    return jax.shard_map(body, mesh=mesh, in_specs=in_specs, out_specs=out_specs, check_vma=False)
```

```python
import functools

import jax
import jax.numpy as jnp
from jax import lax
from jax.experimental import pallas as pl
from jax.experimental.pallas import tpu as pltpu
from jax.sharding import PartitionSpec as P

HEAD_DIM = 128
MESH = pl.DeviceIdType.MESH
F32 = jnp.float32
BF16 = jnp.bfloat16
VMEM_LIMIT = 60 * 1024 * 1024
NT = (((1,), (1,)), ((), ()))
TN = (((0,), (0,)), ((), ()))
EXTRA = 16
STEPS = 32000.0


def place_of(index, n):
    side = index % 2
    row = index // 2
    return row + side * (n - 1 - 2 * row)


def index_at(place, n):
    place = (place + 2 * n) % n
    back = place // (n // 2)
    return 2 * (place + back * (n - 1 - 2 * place)) + back


def enter(peers):
    barrier = pltpu.get_barrier_semaphore()
    for peer in peers:
        pl.semaphore_signal(barrier, inc=1, device_id=peer, device_id_type=MESH)
    pl.semaphore_wait(barrier, len(peers))


class Ring:
    def __init__(self, buf, send, recv, n):
        self.buf, self.send, self.recv, self.n = buf, send, recv, n
        self.place = place_of(lax.axis_index("dp"), n)
        self.copies = []

    def owner(self, way, step):
        return index_at(self.place - step if way == 0 else self.place + step, self.n)

    def pieces(self, way, step):
        if step < self.n // 2 - 1:
            return (0, 1) if way == 0 else (1, 0)
        return (way,)

    def copy(self, way, step, piece):
        to = index_at(self.place + 1 if way == 0 else self.place - 1, self.n)
        block = self.buf.at[2 * self.owner(way, step) + piece]
        return pltpu.make_async_remote_copy(
            src_ref=block,
            dst_ref=block,
            send_sem=self.send.at[way, step, piece],
            recv_sem=self.recv.at[way, step, piece],
            device_id={"dp": to},
            device_id_type=MESH,
        )

    def landed(self, way, step, piece):
        block = self.buf.at[2 * self.owner(way, step + 1) + piece]
        pltpu.make_async_remote_copy(
            src_ref=block,
            dst_ref=block,
            send_sem=self.send.at[way, step, piece],
            recv_sem=self.recv.at[way, step, piece],
            device_id={"dp": self.owner(1, 1)},
            device_id_type=MESH,
        ).wait_recv()

    def run(self, use):
        last = self.n // 2
        for step in range(last + 1):
            for order in range(2):
                for way in range(2):
                    if step > 0:
                        came = self.pieces(way, step - 1)
                        if order < len(came):
                            self.landed(way, step - 1, came[order])
                    if step < last:
                        going = self.pieces(way, step)
                        if order < len(going):
                            copy = self.copy(way, step, going[order])
                            copy.start()
                            self.copies.append(copy)
            if step == 0 or step == last:
                use([self.owner(0, step)], step)
            else:
                use([self.owner(0, step), self.owner(1, step)], step)

    def finish(self):
        for copy in self.copies:
            copy.wait_send()


def attend_one(c, k, group, length, kp, vp, ko, vo, q, cot, att, gq):
    slots = ko.shape[0]
    scale = HEAD_DIM ** (-0.5)
    live = lax.broadcasted_iota(jnp.int32, (slots, HEAD_DIM), 0) < length
    cols = group * slots
    key_id = lax.broadcasted_iota(jnp.int32, (slots, cols), 0)
    row_id = lax.broadcasted_iota(jnp.int32, (slots, cols), 1) % slots
    allowed = key_id <= row_id
    heads = [slice((k * group + g) * HEAD_DIM, (k * group + g + 1) * HEAD_DIM) for g in range(group)]
    qk = jnp.concatenate([q[c, :, h] for h in heads], axis=0)
    do = jnp.concatenate([jnp.where(live, cot[c, :, h].astype(F32), 0.0).astype(BF16) for h in heads], axis=0)
    sp = lax.dot_general(kp, qk, NT, preferred_element_type=F32)
    so = lax.dot_general(ko, qk, NT, preferred_element_type=F32)
    so = jnp.where(allowed, so, -1e30)
    top = jnp.maximum(jnp.max(sp, axis=0, keepdims=True), jnp.max(so, axis=0, keepdims=True))
    ep = jnp.exp((sp - top) * scale)
    eo = jnp.exp((so - top) * scale)
    inv = 1.0 / (jnp.sum(ep, axis=0, keepdims=True) + jnp.sum(eo, axis=0, keepdims=True))
    pp = ep * inv
    po = eo * inv
    wp = pp.astype(BF16)
    wo = po.astype(BF16)
    dp = lax.dot_general(vp, do, NT, preferred_element_type=F32)
    dn = lax.dot_general(vo, do, NT, preferred_element_type=F32)
    delta = jnp.sum(pp * dp, axis=0, keepdims=True) + jnp.sum(po * dn, axis=0, keepdims=True)
    gp = (pp * (dp - delta) * scale).astype(BF16)
    go = (po * (dn - delta) * scale).astype(BF16)
    mixed = lax.dot_general(vp, wp, TN, preferred_element_type=F32) + lax.dot_general(
        vo, wo, TN, preferred_element_type=F32
    )
    dq = lax.dot_general(kp, gp, TN, preferred_element_type=F32) + lax.dot_general(
        ko, go, TN, preferred_element_type=F32
    )
    mixed = mixed.T
    dq = dq.T
    for g, h in enumerate(heads):
        rows = slice(g * slots, (g + 1) * slots)
        att[c, :, h] = jnp.where(live, mixed[rows], 0.0).astype(BF16)
        gq[c, :, h] = dq[rows].astype(BF16)
    return (
        jnp.dot(gp, qk, preferred_element_type=F32).astype(BF16),
        jnp.dot(wp, do, preferred_element_type=F32).astype(BF16),
        jnp.dot(go, qk, preferred_element_type=F32).astype(BF16),
        jnp.dot(wo, do, preferred_element_type=F32).astype(BF16),
    )


def layer_kernel(
    n, per, kv_heads, prompt_of, which, marks, lens, w_ref, ph_hbm, oh_hbm, q_hbm, cot_hbm,
    att_hbm, gq_hbm, wall_hbm, g_ref, *scratch,
):
    ph_ref, oh_ref, q, cot, att, gq, wall_ref, acc, own_kv = scratch[:9]
    pkv, terms, leave, got = (scratch[9 + i * kv_heads : 9 + (i + 1) * kv_heads] for i in range(4))
    load, store, here, send_w, recv_w, send_k, recv_k, send_t, recv_t = scratch[9 + 4 * kv_heads :]
    me = lax.axis_index("dp")
    place = place_of(me, n)
    depth = w_ref.shape[0]
    rows = ph_ref.shape[0]
    plen = rows // per
    comps, slots, features = q.shape
    width = w_ref.shape[1] // 2
    group = features // HEAD_DIM // kv_heads
    tile = min(256, rows)
    last = n // 2
    loads = [
        pltpu.make_async_copy(src, dst, load.at[i])
        for i, (src, dst) in enumerate(((ph_hbm, ph_ref), (oh_hbm, oh_ref), (q_hbm, q), (cot_hbm, cot)))
    ]
    for one in loads:
        one.start()
    wall_ref[2 * me] = w_ref[: depth // 2]
    wall_ref[2 * me + 1] = w_ref[depth // 2 :]
    peers = [index_at(place + d, n) for d in range(1, n)]
    enter([{"dp": peer} for peer in peers])
    ring = Ring(wall_ref, send_w, recv_w, n)

    def add(owners, step):
        if step == 0:
            for one in loads:
                one.wait()
        for source, base in ((ph_ref, 0), (oh_ref, rows)):

            @pl.loop(0, rows // tile)
            def _(r):
                at = pl.multiple_of(r * tile, tile)
                total = None
                for owner in owners:
                    cols = pl.ds(pl.multiple_of(owner * depth, 128), depth)
                    term = jnp.dot(
                        source[pl.ds(at, tile), cols],
                        wall_ref[pl.ds(2 * owner, 2)].reshape(depth, 2 * width),
                        preferred_element_type=F32,
                    )
                    total = term if total is None else total + term
                to = pl.ds(base + at, tile)
                if step == 0:
                    acc[to] = total
                else:
                    acc[to] += total

    ring.run(add)
    wall_out = pltpu.make_async_copy(wall_ref, wall_hbm, store.at[0])
    wall_out.start()

    def head_cols(k):
        return slice(k * HEAD_DIM, (k + 1) * HEAD_DIM), slice(width + k * HEAD_DIM, width + (k + 1) * HEAD_DIM)

    for k in range(kv_heads):
        ks, vs = head_cols(k)
        for s in range(per):
            pkv[k][per * me + s, :, :HEAD_DIM] = acc[s * plen : (s + 1) * plen, ks].astype(BF16)
            pkv[k][per * me + s, :, HEAD_DIM:] = acc[s * plen : (s + 1) * plen, vs].astype(BF16)

    def attend(k, first, count):
        ks, vs = head_cols(k)

        @pl.loop(first, first + count)
        def _(c):
            both = pkv[k][prompt_of[c]]
            own = pl.ds(pl.multiple_of(c * slots, slots), slots)
            tk, tv, ok, ov = attend_one(
                c, k, group, lens[c], both[:, :HEAD_DIM], both[:, HEAD_DIM:],
                own_kv[own, ks], own_kv[own, vs], q, cot, att, gq,
            )
            terms[k][c, :, :HEAD_DIM] = tk
            terms[k][c, :, HEAD_DIM:] = tv
            low = pl.ds(pl.multiple_of(rows + c * slots, slots), slots)
            g_ref[low, ks] = ok
            g_ref[low, vs] = ov

    def ready(k):
        for e in range(n):
            leave[k][e, :plen] = terms[k][which[e]]
            leave[k][e, plen:] = jnp.full((EXTRA, 2 * HEAD_DIM), marks[e].astype(F32), F32).astype(BF16)

    order = sorted(range(1, n), key=lambda d: -min(d, n - d))
    swaps = []

    def swap(k):
        for d in order:
            peer = peers[d - 1]
            one = pltpu.make_async_remote_copy(
                src_ref=leave[k].at[peer],
                dst_ref=got[k].at[me],
                send_sem=send_t.at[k, d],
                recv_sem=recv_t.at[k, d],
                device_id={"dp": peer},
                device_id_type=MESH,
            )
            one.start()
            swaps.append(one)

    def collect(k):
        own_copy = pltpu.make_async_copy(leave[k].at[me], got[k].at[me], here)
        own_copy.start()
        own_copy.wait()
        for d in order:
            came = got[k].at[index_at(place - d, n)]
            pltpu.make_async_remote_copy(
                src_ref=came,
                dst_ref=came,
                send_sem=send_t.at[k, d],
                recv_sem=recv_t.at[k, d],
                device_id={"dp": peers[0]},
                device_id_type=MESH,
            ).wait_recv()
        ks, vs = head_cols(k)
        for s in range(per):
            total = jnp.zeros((plen, 2 * HEAD_DIM), F32)
            for e in range(n):
                mark = got[k][e, plen:].astype(F32)[:1]
                total = total + jnp.where(mark == float(s + 1), got[k][e, :plen].astype(F32), 0.0)
            kept = total.astype(BF16)
            g_ref[s * plen : (s + 1) * plen, ks] = kept[:, :HEAD_DIM]
            g_ref[s * plen : (s + 1) * plen, vs] = kept[:, HEAD_DIM:]

    def own_rows(owners, step):
        if step == 0:
            own_kv[...] = acc[rows:].astype(BF16)

    rings = [Ring(pkv[k], send_k.at[k], recv_k.at[k], n) for k in range(kv_heads)]
    share = -(-comps // last)
    for k in range(kv_heads):

        def beside(owners, step, k=k):
            if k == 0:
                own_rows(owners, step)
            elif step < last and step * share < comps:
                attend(k - 1, step * share, min(share, comps - step * share))

        rings[k].run(beside)
        if k > 0:
            ready(k - 1)
            swap(k - 1)
    attend(kv_heads - 1, 0, comps)
    ready(kv_heads - 1)
    swap(kv_heads - 1)
    outs = [pltpu.make_async_copy(att, att_hbm, store.at[1]), pltpu.make_async_copy(gq, gq_hbm, store.at[2])]
    for one in outs:
        one.start()
    for k in range(kv_heads):
        collect(k)
    wall_out.wait()
    for one in outs:
        one.wait()
    for one in [ring] + rings:
        one.finish()
    for one in swaps:
        one.wait_send()


def layer(prompt_of, lens, w, ph, oh, q, cot, n, per):
    depth, width = w.shape
    rows = ph.shape[0]
    plen = rows // per
    comps = q.shape[0]
    kv_heads = width // (2 * HEAD_DIM)
    hold = 2 * HEAD_DIM
    fits = prompt_of[None, :] // per == jnp.arange(n, dtype=jnp.int32)[:, None]
    which = jnp.sum(jnp.where(fits, jnp.arange(comps, dtype=jnp.int32)[None, :], 0), axis=1)
    marks = jnp.sum(jnp.where(fits, prompt_of[None, :] % per + 1, 0), axis=1)
    vmem = pl.BlockSpec(memory_space=pltpu.VMEM)
    hbm = pl.BlockSpec(memory_space=pl.ANY)
    smem = pl.BlockSpec(memory_space=pltpu.SMEM)
    wide = pltpu.VMEM(q.shape, BF16)
    sems = pltpu.SemaphoreType.DMA((2, n // 2, 2))
    more = pltpu.SemaphoreType.DMA((kv_heads, 2, n // 2, 2))
    swap_sems = pltpu.SemaphoreType.DMA((kv_heads, n))
    return pl.pallas_call(
        functools.partial(layer_kernel, n, per, kv_heads),
        out_shape=(
            jax.ShapeDtypeStruct(q.shape, BF16),
            jax.ShapeDtypeStruct(q.shape, BF16),
            jax.ShapeDtypeStruct((2 * n, depth // 2, width), BF16),
            jax.ShapeDtypeStruct((rows + oh.shape[0], width), BF16),
        ),
        in_specs=[smem] * 4 + [vmem] + [hbm] * 4,
        out_specs=(hbm, hbm, hbm, vmem),
        scratch_shapes=[
            pltpu.VMEM(ph.shape, BF16),
            pltpu.VMEM(oh.shape, BF16),
            wide,
            wide,
            wide,
            wide,
            pltpu.VMEM((2 * n, depth // 2, width), BF16),
            pltpu.VMEM((rows + oh.shape[0], width), F32),
            pltpu.VMEM((oh.shape[0], width), BF16),
        ]
        + [pltpu.VMEM((n * per, plen, hold), BF16)] * kv_heads
        + [pltpu.VMEM((comps, plen, hold), BF16)] * kv_heads
        + [pltpu.VMEM((n, plen + EXTRA, hold), BF16)] * (2 * kv_heads)
        + [
            pltpu.SemaphoreType.DMA((4,)),
            pltpu.SemaphoreType.DMA((3,)),
            pltpu.SemaphoreType.DMA,
            sems,
            sems,
            more,
            more,
            swap_sems,
            swap_sems,
        ],
        compiler_params=pltpu.CompilerParams(collective_id=0, has_side_effects=True, vmem_limit_bytes=VMEM_LIMIT),
        name="layer",
    )(prompt_of, which, marks, lens, w, ph, oh, q, cot)


def encode(block, ref):
    top = jnp.maximum(jnp.max(jnp.abs(block), axis=0, keepdims=True), 1e-30)
    power = jnp.ceil(jnp.log2(top))
    rows = block.shape[0]
    ref[:rows] = jnp.round(block * (jnp.exp2(-power) * STEPS)).astype(jnp.int32).astype(jnp.int16)
    ref[rows:] = jnp.broadcast_to(power, (EXTRA, block.shape[1])).astype(jnp.int32).astype(jnp.int16)


def decode(ref):
    rows = ref.shape[0] - EXTRA
    power = ref[rows:].astype(jnp.int32).astype(F32)[:1]
    return ref[:rows].astype(jnp.int32).astype(F32) * (jnp.exp2(power) * (1.0 / STEPS))


def grads_kernel(
    n, chunk, g_ref, ph_hbm, oh_hbm, wall_hbm, fp_ref, fo_ref, gw_ref,
    gt_ref, ph_ref, oh_ref, wall_ref, slots, fsend, frecv, load, send, recv, send_f, recv_f,
):
    me = lax.axis_index("dp")
    mp = lax.axis_index("mp")
    place = place_of(me, n)
    right = index_at(place + 1, n)
    left = index_at(place - 1, n)
    other = {"mp": 1 - mp}
    rows = ph_ref.shape[0]
    depth = gw_ref.shape[0]
    width = gt_ref.shape[0]
    half = width // 2
    last = n // 2
    chunks = fsend.shape[1]
    tile = min(256, rows)
    loads = [
        pltpu.make_async_copy(src, dst, load.at[i])
        for i, (src, dst) in enumerate(((oh_hbm, oh_ref), (ph_hbm, ph_ref), (wall_hbm, wall_ref)))
    ]
    for one in loads:
        one.start()
    enter([{"dp": right}, {"dp": left}, other])
    span = chunk * chunks

    def product(first, at):
        return lax.dot_general(
            g_ref[pl.ds(at, tile)], wall_ref[pl.ds(first, chunk)], NT, preferred_element_type=F32
        ).astype(BF16)

    feature = {}

    def away(part):
        for j in range(chunks):
            first = pl.multiple_of((1 - mp) * span + j * chunk, 128)

            @pl.loop(0, rows // tile)
            def _(r):
                at = pl.multiple_of(r * tile, tile)
                fsend[part, j, pl.ds(at, tile)] = product(first, pl.multiple_of(part * rows + at, tile))

            one = pltpu.make_async_remote_copy(
                src_ref=fsend.at[part, j],
                dst_ref=frecv.at[part, j],
                send_sem=send_f.at[part, j],
                recv_sem=recv_f.at[part, j],
                device_id=other,
                device_id_type=MESH,
            )
            one.start()
            feature[part, j] = one

    def home(part, out_ref):
        for j in range(chunks):
            first = pl.multiple_of(mp * span + j * chunk, 128)
            feature[part, j].wait_recv()

            @pl.loop(0, rows // tile)
            def _(r):
                at = pl.multiple_of(r * tile, tile)
                mine = product(first, pl.multiple_of(part * rows + at, tile)).astype(F32)
                total = mine + frecv[part, j, pl.ds(at, tile)].astype(F32)
                out_ref[pl.ds(at, tile), j * chunk : (j + 1) * chunk] = total.astype(BF16)

    for lane in range(0, width, half):
        gt_ref[lane : lane + half] = g_ref[:, lane : lane + half].astype(F32).T.astype(BF16)
    loads[0].wait()
    loads[1].wait()

    def partial(target, piece):
        cols = pl.ds(pl.multiple_of(target * depth, 128), depth)
        top = gt_ref[piece * half : (piece + 1) * half]
        return jnp.dot(top[:, :rows], ph_ref[:, cols], preferred_element_type=F32) + jnp.dot(
            top[:, rows:], oh_ref[:, cols], preferred_element_type=F32
        )

    def copy(way, step, piece):
        return pltpu.make_async_remote_copy(
            src_ref=slots.at[way, step, piece],
            dst_ref=slots.at[way, step + 1, piece],
            send_sem=send.at[way, step, piece],
            recv_sem=recv.at[way, step, piece],
            device_id={"dp": right if way == 0 else left},
            device_id_type=MESH,
        )

    started = []

    def go(way, step, piece):
        one = copy(way, step, piece)
        one.start()
        started.append(one)

    far = index_at(place + last, n)
    for way in range(2):
        encode(partial(far, way), slots.at[way, 0, way])
        go(way, 0, way)
    for way in range(2):
        near = index_at(place + (last - 1) if way == 0 else place - (last - 1), n)
        encode(partial(near, 1 - way), slots.at[way, 1, 1 - way])
        go(way, 1, 1 - way)
    loads[2].wait()
    away(0)
    away(1)
    for step in range(1, last):
        for turn in range(2):
            for way in range(2):
                piece = way if turn == 0 else 1 - way
                if step == 1 and piece != way:
                    continue
                target = index_at(place + (last - step) if way == 0 else place - (last - step), n)
                mine = partial(target, piece)
                copy(way, step - 1, piece).wait_recv()
                encode(decode(slots.at[way, step, piece]) + mine, slots.at[way, step, piece])
                go(way, step, piece)
        if step == 1:
            home(0, fp_ref)
        if step == min(2, last - 1):
            home(1, fo_ref)
    for piece in range(2):
        mine = partial(me, piece)
        for way in range(2):
            copy(way, last - 1, piece).wait_recv()
        total = mine + decode(slots.at[0, last, piece]) + decode(slots.at[1, last, piece])
        gw_ref[:, piece * half : (piece + 1) * half] = total.T
    for one in started + list(feature.values()):
        one.wait_send()


def grads(g, ph, oh, wall, n, n_mp):
    rows, model_dim = ph.shape
    width = g.shape[1]
    depth = model_dim // n
    share = model_dim // n_mp
    chunk = 512 if share % 512 == 0 else 128
    chunks = share // chunk
    vmem = pl.BlockSpec(memory_space=pltpu.VMEM)
    hbm = pl.BlockSpec(memory_space=pl.ANY)
    sems = pltpu.SemaphoreType.DMA((2, n // 2, 2))
    return pl.pallas_call(
        functools.partial(grads_kernel, n, chunk),
        out_shape=(
            jax.ShapeDtypeStruct((rows, share), BF16),
            jax.ShapeDtypeStruct((rows, share), BF16),
            jax.ShapeDtypeStruct((depth, width), F32),
        ),
        in_specs=[vmem, hbm, hbm, hbm],
        out_specs=(vmem,) * 3,
        scratch_shapes=[
            pltpu.VMEM((width, 2 * rows), BF16),
            pltpu.VMEM(ph.shape, BF16),
            pltpu.VMEM(oh.shape, BF16),
            pltpu.VMEM(wall.shape, BF16),
            pltpu.VMEM((2, n // 2 + 1, 2, width // 2 + EXTRA, depth), jnp.int16),
            pltpu.VMEM((2, chunks, rows, chunk), BF16),
            pltpu.VMEM((2, chunks, rows, chunk), BF16),
            pltpu.SemaphoreType.DMA((3,)),
            sems,
            sems,
            pltpu.SemaphoreType.DMA((2, chunks)),
            pltpu.SemaphoreType.DMA((2, chunks)),
        ],
        compiler_params=pltpu.CompilerParams(collective_id=2, has_side_effects=True, vmem_limit_bytes=VMEM_LIMIT),
        name="grads_reduce",
    )(g, ph, oh, wall)


def shards(n, n_mp, prompt_hidden, completion_hidden, queries, cotangent, kv_weight, prompt_of, comp_len):
    per, plen, model_dim = prompt_hidden.shape
    comps, slots, _ = completion_hidden.shape
    depth, _, kv_width = kv_weight.shape
    width = 2 * kv_width
    w = kv_weight.reshape(depth, width)
    ph = prompt_hidden.reshape(per * plen, model_dim)
    oh = completion_hidden.reshape(comps * slots, model_dim)
    attended, grad_queries, wall, g = layer(
        prompt_of, comp_len.reshape(-1), w, ph, oh, queries, cotangent, n, per
    )
    fp, fo, gw = grads(g, ph, oh, wall.reshape(model_dim, width), n, n_mp)
    return (
        attended,
        grad_queries,
        fp.reshape(per, plen, -1),
        fo.reshape(comps, slots, -1),
        gw.reshape(depth, 2, kv_width),
    )


def solution(mesh):
    in_specs = (
        P(("groups", "dp"), None, None),
        P(("groups", "dp"), None, None),
        P(("groups", "dp"), None, "mp"),
        P(("groups", "dp"), None, "mp"),
        P("dp", None, "mp"),
        P(("groups", "dp")),
        P(("groups", "dp"), None),
    )
    out_specs = (P(("groups", "dp"), None, "mp"),) * 5
    body = functools.partial(shards, mesh.shape["dp"], mesh.shape["mp"])
    return jax.shard_map(body, mesh=mesh, in_specs=in_specs, out_specs=out_specs, check_vma=False)
```

```python
import functools

import jax
import jax.numpy as jnp
from jax import lax
from jax.experimental import pallas as pl
from jax.experimental.pallas import tpu as pltpu
from jax.sharding import PartitionSpec as P

HEAD_DIM = 128
MESH = pl.DeviceIdType.MESH
F32 = jnp.float32
BF16 = jnp.bfloat16
VMEM_LIMIT = 60 * 1024 * 1024
NT = (((1,), (1,)), ((), ()))
TN = (((0,), (0,)), ((), ()))
EXTRA = 16
STEPS = 32000.0


def place_of(index, n):
    side = index % 2
    row = index // 2
    return row + side * (n - 1 - 2 * row)


def index_at(place, n):
    place = (place + 2 * n) % n
    back = place // (n // 2)
    return 2 * (place + back * (n - 1 - 2 * place)) + back


def enter(peers):
    barrier = pltpu.get_barrier_semaphore()
    for peer in peers:
        pl.semaphore_signal(barrier, inc=1, device_id=peer, device_id_type=MESH)
    pl.semaphore_wait(barrier, len(peers))


class Ring:
    def __init__(self, block, send, recv, n):
        self.block, self.send, self.recv, self.n = block, send, recv, n
        self.place = place_of(lax.axis_index("dp"), n)
        self.copies = []

    def owner(self, way, step):
        return index_at(self.place - step if way == 0 else self.place + step, self.n)

    def pieces(self, way, step):
        if step < self.n // 2 - 1:
            return (0, 1) if way == 0 else (1, 0)
        return (way,)

    def copy(self, way, step, piece):
        to = index_at(self.place + 1 if way == 0 else self.place - 1, self.n)
        block = self.block(self.owner(way, step), piece)
        return pltpu.make_async_remote_copy(
            src_ref=block,
            dst_ref=block,
            send_sem=self.send.at[way, step, piece],
            recv_sem=self.recv.at[way, step, piece],
            device_id={"dp": to},
            device_id_type=MESH,
        )

    def landed(self, way, step, piece):
        block = self.block(self.owner(way, step + 1), piece)
        pltpu.make_async_remote_copy(
            src_ref=block,
            dst_ref=block,
            send_sem=self.send.at[way, step, piece],
            recv_sem=self.recv.at[way, step, piece],
            device_id={"dp": self.owner(1, 1)},
            device_id_type=MESH,
        ).wait_recv()

    def run(self, use):
        last = self.n // 2
        for step in range(last + 1):
            for order in range(2):
                for way in range(2):
                    if step > 0:
                        came = self.pieces(way, step - 1)
                        if order < len(came):
                            self.landed(way, step - 1, came[order])
                    if step < last:
                        going = self.pieces(way, step)
                        if order < len(going):
                            copy = self.copy(way, step, going[order])
                            copy.start()
                            self.copies.append(copy)
            if step == 0 or step == last:
                use([self.owner(0, step)], step)
            else:
                use([self.owner(0, step), self.owner(1, step)], step)

    def finish(self):
        for copy in self.copies:
            copy.wait_send()


def attend_one(c, k, group, length, kp, vp, ko, vo, q, cot, att, gq):
    slots = ko.shape[0]
    scale = HEAD_DIM ** (-0.5)
    live = lax.broadcasted_iota(jnp.int32, (slots, HEAD_DIM), 0) < length
    cols = group * slots
    key_id = lax.broadcasted_iota(jnp.int32, (slots, cols), 0)
    row_id = lax.broadcasted_iota(jnp.int32, (slots, cols), 1) % slots
    allowed = key_id <= row_id
    heads = [slice((k * group + g) * HEAD_DIM, (k * group + g + 1) * HEAD_DIM) for g in range(group)]
    qk = jnp.concatenate([q[c, :, h] for h in heads], axis=0)
    do = jnp.concatenate([jnp.where(live, cot[c, :, h].astype(F32), 0.0).astype(BF16) for h in heads], axis=0)
    sp = lax.dot_general(kp, qk, NT, preferred_element_type=F32)
    so = lax.dot_general(ko, qk, NT, preferred_element_type=F32)
    so = jnp.where(allowed, so, -1e30)
    top = jnp.maximum(jnp.max(sp, axis=0, keepdims=True), jnp.max(so, axis=0, keepdims=True))
    ep = jnp.exp((sp - top) * scale)
    eo = jnp.exp((so - top) * scale)
    inv = 1.0 / (jnp.sum(ep, axis=0, keepdims=True) + jnp.sum(eo, axis=0, keepdims=True))
    pp = ep * inv
    po = eo * inv
    wp = pp.astype(BF16)
    wo = po.astype(BF16)
    dp = lax.dot_general(vp, do, NT, preferred_element_type=F32)
    dn = lax.dot_general(vo, do, NT, preferred_element_type=F32)
    delta = jnp.sum(pp * dp, axis=0, keepdims=True) + jnp.sum(po * dn, axis=0, keepdims=True)
    gp = (pp * (dp - delta) * scale).astype(BF16)
    go = (po * (dn - delta) * scale).astype(BF16)
    mixed = lax.dot_general(vp, wp, TN, preferred_element_type=F32) + lax.dot_general(
        vo, wo, TN, preferred_element_type=F32
    )
    dq = lax.dot_general(kp, gp, TN, preferred_element_type=F32) + lax.dot_general(
        ko, go, TN, preferred_element_type=F32
    )
    mixed = mixed.T
    dq = dq.T
    for g, h in enumerate(heads):
        rows = slice(g * slots, (g + 1) * slots)
        att[c, :, h] = jnp.where(live, mixed[rows], 0.0).astype(BF16)
        gq[c, :, h] = dq[rows].astype(BF16)
    return (
        jnp.dot(gp, qk, preferred_element_type=F32).astype(BF16),
        jnp.dot(wp, do, preferred_element_type=F32).astype(BF16),
        jnp.dot(go, qk, preferred_element_type=F32).astype(BF16),
        jnp.dot(wo, do, preferred_element_type=F32).astype(BF16),
    )


def layer_kernel(
    n, per, kv_heads, prompt_of, which, marks, lens, w_ref, ph_hbm, oh_hbm, q_hbm, cot_hbm,
    att_hbm, gq_hbm, wall_hbm, g_ref, *scratch,
):
    ph_ref, oh_ref, q, cot, att, gq, wall_ref, acc, own_kv = scratch[:9]
    pkv, terms, leave, got = (scratch[9 + i * kv_heads : 9 + (i + 1) * kv_heads] for i in range(4))
    load, store, here, send_w, recv_w, send_x, recv_x, send_k, recv_k, send_t, recv_t = scratch[9 + 4 * kv_heads :]
    me = lax.axis_index("dp")
    place = place_of(me, n)
    depth = w_ref.shape[0]
    rows = ph_ref.shape[0]
    plen = rows // per
    comps, slots, features = q.shape
    width = w_ref.shape[1] // 2
    group = features // HEAD_DIM // kv_heads
    tile = min(256, rows)
    last = n // 2
    loads = [
        pltpu.make_async_copy(src, dst, load.at[i])
        for i, (src, dst) in enumerate(((ph_hbm, ph_ref), (oh_hbm, oh_ref), (q_hbm, q), (cot_hbm, cot)))
    ]
    for one in loads:
        one.start()
    wall_ref[me] = w_ref[...]
    peers = [index_at(place + d, n) for d in range(1, n)]
    group_id = lax.axis_index("groups")
    side = group_id % 2
    twin = {"groups": group_id + 1 - 2 * side}
    enter([{"dp": peer} for peer in peers] + [twin])
    skip = depth * 3 // 10 // 32 * 32
    piece_rows = (depth - skip) // 2
    ring = Ring(
        lambda owner, piece: wall_ref.at[owner, pl.ds(pl.multiple_of(side * skip + piece * piece_rows, 16), piece_rows)],
        send_w, recv_w, n,
    )

    def across(owner, way, step):
        rows_out = pl.ds(pl.multiple_of(side * (depth - skip), 16), skip)
        return pltpu.make_async_remote_copy(
            src_ref=wall_ref.at[owner, rows_out],
            dst_ref=wall_ref.at[owner, rows_out],
            send_sem=send_x.at[way, step],
            recv_sem=recv_x.at[way, step],
            device_id=twin,
            device_id_type=MESH,
        )

    def crossed(owner, way, step):
        rows_in = wall_ref.at[owner, pl.ds(pl.multiple_of((1 - side) * (depth - skip), 16), skip)]
        pltpu.make_async_remote_copy(
            src_ref=rows_in,
            dst_ref=rows_in,
            send_sem=send_x.at[way, step],
            recv_sem=recv_x.at[way, step],
            device_id=twin,
            device_id_type=MESH,
        ).wait_recv()

    def add(owners, step):
        if step == 0:
            for one in loads:
                one.wait()
        for source, base in ((ph_ref, 0), (oh_ref, rows)):

            @pl.loop(0, rows // tile)
            def _(r):
                at = pl.multiple_of(r * tile, tile)
                total = None
                for owner in owners:
                    cols = pl.ds(pl.multiple_of(owner * depth, 128), depth)
                    term = jnp.dot(
                        source[pl.ds(at, tile), cols],
                        wall_ref[owner],
                        preferred_element_type=F32,
                    )
                    total = term if total is None else total + term
                to = pl.ds(base + at, tile)
                if step == 0:
                    acc[to] = total
                else:
                    acc[to] += total

    pending, crossing = [], []

    def finish_pending():
        if pending:
            owners, step = pending.pop()
            for way, owner in enumerate(owners):
                crossed(owner, way, step)
            add(owners, step)

    def gathered(owners, step):
        if step == 0:
            add(owners, step)
            return
        for way, owner in enumerate(owners):
            one = across(owner, way, step)
            one.start()
            crossing.append(one)
        finish_pending()
        pending.append((owners, step))

    ring.run(gathered)
    finish_pending()
    wall_out = pltpu.make_async_copy(wall_ref, wall_hbm, store.at[0])
    wall_out.start()

    def head_cols(k):
        return slice(k * HEAD_DIM, (k + 1) * HEAD_DIM), slice(width + k * HEAD_DIM, width + (k + 1) * HEAD_DIM)

    for k in range(kv_heads):
        ks, vs = head_cols(k)
        for s in range(per):
            pkv[k][per * me + s, :, :HEAD_DIM] = acc[s * plen : (s + 1) * plen, ks].astype(BF16)
            pkv[k][per * me + s, :, HEAD_DIM:] = acc[s * plen : (s + 1) * plen, vs].astype(BF16)

    def attend(k, first, count):
        ks, vs = head_cols(k)

        @pl.loop(first, first + count)
        def _(c):
            both = pkv[k][prompt_of[c]]
            own = pl.ds(pl.multiple_of(c * slots, slots), slots)
            tk, tv, ok, ov = attend_one(
                c, k, group, lens[c], both[:, :HEAD_DIM], both[:, HEAD_DIM:],
                own_kv[own, ks], own_kv[own, vs], q, cot, att, gq,
            )
            terms[k][c, :, :HEAD_DIM] = tk
            terms[k][c, :, HEAD_DIM:] = tv
            low = pl.ds(pl.multiple_of(rows + c * slots, slots), slots)
            g_ref[low, ks] = ok
            g_ref[low, vs] = ov

    def ready(k):
        for e in range(n):
            leave[k][e, :plen] = terms[k][which[e]]
            leave[k][e, plen:] = jnp.full((EXTRA, 2 * HEAD_DIM), marks[e].astype(F32), F32).astype(BF16)

    order = sorted(range(1, n), key=lambda d: -min(d, n - d))
    swaps = []

    def swap(k):
        for d in order:
            peer = peers[d - 1]
            one = pltpu.make_async_remote_copy(
                src_ref=leave[k].at[peer],
                dst_ref=got[k].at[me],
                send_sem=send_t.at[k, d],
                recv_sem=recv_t.at[k, d],
                device_id={"dp": peer},
                device_id_type=MESH,
            )
            one.start()
            swaps.append(one)

    def collect(k):
        own_copy = pltpu.make_async_copy(leave[k].at[me], got[k].at[me], here)
        own_copy.start()
        own_copy.wait()
        for d in order:
            came = got[k].at[index_at(place - d, n)]
            pltpu.make_async_remote_copy(
                src_ref=came,
                dst_ref=came,
                send_sem=send_t.at[k, d],
                recv_sem=recv_t.at[k, d],
                device_id={"dp": peers[0]},
                device_id_type=MESH,
            ).wait_recv()
        ks, vs = head_cols(k)
        for s in range(per):
            total = jnp.zeros((plen, 2 * HEAD_DIM), F32)
            for e in range(n):
                mark = got[k][e, plen:].astype(F32)[:1]
                total = total + jnp.where(mark == float(s + 1), got[k][e, :plen].astype(F32), 0.0)
            kept = total.astype(BF16)
            g_ref[s * plen : (s + 1) * plen, ks] = kept[:, :HEAD_DIM]
            g_ref[s * plen : (s + 1) * plen, vs] = kept[:, HEAD_DIM:]

    def own_rows(owners, step):
        if step == 0:
            own_kv[...] = acc[rows:].astype(BF16)

    rings = [
        Ring(lambda owner, piece, k=k: pkv[k].at[2 * owner + piece], send_k.at[k], recv_k.at[k], n)
        for k in range(kv_heads)
    ]
    share = -(-comps // last)
    for k in range(kv_heads):

        def beside(owners, step, k=k):
            if k == 0:
                own_rows(owners, step)
            elif step < last and step * share < comps:
                attend(k - 1, step * share, min(share, comps - step * share))

        rings[k].run(beside)
        if k > 0:
            ready(k - 1)
            swap(k - 1)
    attend(kv_heads - 1, 0, comps)
    ready(kv_heads - 1)
    swap(kv_heads - 1)
    outs = [pltpu.make_async_copy(att, att_hbm, store.at[1]), pltpu.make_async_copy(gq, gq_hbm, store.at[2])]
    for one in outs:
        one.start()
    for k in range(kv_heads):
        collect(k)
    wall_out.wait()
    for one in outs:
        one.wait()
    for one in [ring] + rings:
        one.finish()
    for one in swaps + crossing:
        one.wait_send()


def layer(prompt_of, lens, w, ph, oh, q, cot, n, per):
    depth, width = w.shape
    rows = ph.shape[0]
    plen = rows // per
    comps = q.shape[0]
    kv_heads = width // (2 * HEAD_DIM)
    hold = 2 * HEAD_DIM
    fits = prompt_of[None, :] // per == jnp.arange(n, dtype=jnp.int32)[:, None]
    which = jnp.sum(jnp.where(fits, jnp.arange(comps, dtype=jnp.int32)[None, :], 0), axis=1)
    marks = jnp.sum(jnp.where(fits, prompt_of[None, :] % per + 1, 0), axis=1)
    vmem = pl.BlockSpec(memory_space=pltpu.VMEM)
    hbm = pl.BlockSpec(memory_space=pl.ANY)
    smem = pl.BlockSpec(memory_space=pltpu.SMEM)
    wide = pltpu.VMEM(q.shape, BF16)
    sems = pltpu.SemaphoreType.DMA((2, n // 2, 2))
    more = pltpu.SemaphoreType.DMA((kv_heads, 2, n // 2, 2))
    swap_sems = pltpu.SemaphoreType.DMA((kv_heads, n))
    return pl.pallas_call(
        functools.partial(layer_kernel, n, per, kv_heads),
        out_shape=(
            jax.ShapeDtypeStruct(q.shape, BF16),
            jax.ShapeDtypeStruct(q.shape, BF16),
            jax.ShapeDtypeStruct((n, depth, width), BF16),
            jax.ShapeDtypeStruct((rows + oh.shape[0], width), BF16),
        ),
        in_specs=[smem] * 4 + [vmem] + [hbm] * 4,
        out_specs=(hbm, hbm, hbm, vmem),
        scratch_shapes=[
            pltpu.VMEM(ph.shape, BF16),
            pltpu.VMEM(oh.shape, BF16),
            wide,
            wide,
            wide,
            wide,
            pltpu.VMEM((n, depth, width), BF16),
            pltpu.VMEM((rows + oh.shape[0], width), F32),
            pltpu.VMEM((oh.shape[0], width), BF16),
        ]
        + [pltpu.VMEM((n * per, plen, hold), BF16)] * kv_heads
        + [pltpu.VMEM((comps, plen, hold), BF16)] * kv_heads
        + [pltpu.VMEM((n, plen + EXTRA, hold), BF16)] * (2 * kv_heads)
        + [
            pltpu.SemaphoreType.DMA((4,)),
            pltpu.SemaphoreType.DMA((3,)),
            pltpu.SemaphoreType.DMA,
            sems,
            sems,
            pltpu.SemaphoreType.DMA((2, n // 2 + 1)),
            pltpu.SemaphoreType.DMA((2, n // 2 + 1)),
            more,
            more,
            swap_sems,
            swap_sems,
        ],
        compiler_params=pltpu.CompilerParams(collective_id=0, has_side_effects=True, vmem_limit_bytes=VMEM_LIMIT),
        name="layer",
    )(prompt_of, which, marks, lens, w, ph, oh, q, cot)


def encode(block, ref):
    top = jnp.maximum(jnp.max(jnp.abs(block), axis=0, keepdims=True), 1e-30)
    power = jnp.ceil(jnp.log2(top))
    rows = block.shape[0]
    ref[:rows] = jnp.round(block * (jnp.exp2(-power) * STEPS)).astype(jnp.int32).astype(jnp.int16)
    ref[rows:] = jnp.broadcast_to(power, (EXTRA, block.shape[1])).astype(jnp.int32).astype(jnp.int16)


def decode(ref):
    rows = ref.shape[0] - EXTRA
    power = ref[rows:].astype(jnp.int32).astype(F32)[:1]
    return ref[:rows].astype(jnp.int32).astype(F32) * (jnp.exp2(power) * (1.0 / STEPS))


def grads_kernel(
    n, chunk, g_ref, ph_hbm, oh_hbm, wall_hbm, fp_ref, fo_ref, gw_ref,
    gt_ref, ph_ref, oh_ref, wall_ref, slots, fsend, frecv, load, send, recv, send_f, recv_f,
):
    me = lax.axis_index("dp")
    mp = lax.axis_index("mp")
    place = place_of(me, n)
    right = index_at(place + 1, n)
    left = index_at(place - 1, n)
    other = {"mp": 1 - mp}
    rows = ph_ref.shape[0]
    depth = gw_ref.shape[0]
    width = gt_ref.shape[0]
    half = width // 2
    last = n // 2
    chunks = fsend.shape[1]
    tile = min(256, rows)
    loads = [
        pltpu.make_async_copy(src, dst, load.at[i])
        for i, (src, dst) in enumerate(((oh_hbm, oh_ref), (ph_hbm, ph_ref), (wall_hbm, wall_ref)))
    ]
    for one in loads:
        one.start()
    enter([{"dp": right}, {"dp": left}, other])
    span = chunk * chunks

    def product(first, at):
        return lax.dot_general(
            g_ref[pl.ds(at, tile)], wall_ref[pl.ds(first, chunk)], NT, preferred_element_type=F32
        ).astype(BF16)

    feature = {}

    def away(part):
        for j in range(chunks):
            first = pl.multiple_of((1 - mp) * span + j * chunk, 128)

            @pl.loop(0, rows // tile)
            def _(r):
                at = pl.multiple_of(r * tile, tile)
                fsend[part, j, pl.ds(at, tile)] = product(first, pl.multiple_of(part * rows + at, tile))

            one = pltpu.make_async_remote_copy(
                src_ref=fsend.at[part, j],
                dst_ref=frecv.at[part, j],
                send_sem=send_f.at[part, j],
                recv_sem=recv_f.at[part, j],
                device_id=other,
                device_id_type=MESH,
            )
            one.start()
            feature[part, j] = one

    def home(part, out_ref):
        for j in range(chunks):
            first = pl.multiple_of(mp * span + j * chunk, 128)
            feature[part, j].wait_recv()

            @pl.loop(0, rows // tile)
            def _(r):
                at = pl.multiple_of(r * tile, tile)
                mine = product(first, pl.multiple_of(part * rows + at, tile)).astype(F32)
                total = mine + frecv[part, j, pl.ds(at, tile)].astype(F32)
                out_ref[pl.ds(at, tile), j * chunk : (j + 1) * chunk] = total.astype(BF16)

    for lane in range(0, width, half):
        gt_ref[lane : lane + half] = g_ref[:, lane : lane + half].astype(F32).T.astype(BF16)
    loads[0].wait()
    loads[1].wait()

    def partial(target, piece):
        cols = pl.ds(pl.multiple_of(target * depth, 128), depth)
        top = gt_ref[piece * half : (piece + 1) * half]
        return jnp.dot(top[:, :rows], ph_ref[:, cols], preferred_element_type=F32) + jnp.dot(
            top[:, rows:], oh_ref[:, cols], preferred_element_type=F32
        )

    def copy(way, step, piece):
        return pltpu.make_async_remote_copy(
            src_ref=slots.at[way, step, piece],
            dst_ref=slots.at[way, step + 1, piece],
            send_sem=send.at[way, step, piece],
            recv_sem=recv.at[way, step, piece],
            device_id={"dp": right if way == 0 else left},
            device_id_type=MESH,
        )

    started = []

    def go(way, step, piece):
        one = copy(way, step, piece)
        one.start()
        started.append(one)

    far = index_at(place + last, n)
    for way in range(2):
        encode(partial(far, way), slots.at[way, 0, way])
        go(way, 0, way)
    for way in range(2):
        near = index_at(place + (last - 1) if way == 0 else place - (last - 1), n)
        encode(partial(near, 1 - way), slots.at[way, 1, 1 - way])
        go(way, 1, 1 - way)
    loads[2].wait()
    away(0)
    away(1)
    for step in range(1, last):
        for turn in range(2):
            for way in range(2):
                piece = way if turn == 0 else 1 - way
                if step == 1 and piece != way:
                    continue
                target = index_at(place + (last - step) if way == 0 else place - (last - step), n)
                mine = partial(target, piece)
                copy(way, step - 1, piece).wait_recv()
                encode(decode(slots.at[way, step, piece]) + mine, slots.at[way, step, piece])
                go(way, step, piece)
        if step == 1:
            home(0, fp_ref)
        if step == min(2, last - 1):
            home(1, fo_ref)
    for piece in range(2):
        mine = partial(me, piece)
        for way in range(2):
            copy(way, last - 1, piece).wait_recv()
        total = mine + decode(slots.at[0, last, piece]) + decode(slots.at[1, last, piece])
        gw_ref[:, piece * half : (piece + 1) * half] = total.T
    for one in started + list(feature.values()):
        one.wait_send()


def grads(g, ph, oh, wall, n, n_mp):
    rows, model_dim = ph.shape
    width = g.shape[1]
    depth = model_dim // n
    share = model_dim // n_mp
    chunk = 512 if share % 512 == 0 else 128
    chunks = share // chunk
    vmem = pl.BlockSpec(memory_space=pltpu.VMEM)
    hbm = pl.BlockSpec(memory_space=pl.ANY)
    sems = pltpu.SemaphoreType.DMA((2, n // 2, 2))
    return pl.pallas_call(
        functools.partial(grads_kernel, n, chunk),
        out_shape=(
            jax.ShapeDtypeStruct((rows, share), BF16),
            jax.ShapeDtypeStruct((rows, share), BF16),
            jax.ShapeDtypeStruct((depth, width), F32),
        ),
        in_specs=[vmem, hbm, hbm, hbm],
        out_specs=(vmem,) * 3,
        scratch_shapes=[
            pltpu.VMEM((width, 2 * rows), BF16),
            pltpu.VMEM(ph.shape, BF16),
            pltpu.VMEM(oh.shape, BF16),
            pltpu.VMEM(wall.shape, BF16),
            pltpu.VMEM((2, n // 2 + 1, 2, width // 2 + EXTRA, depth), jnp.int16),
            pltpu.VMEM((2, chunks, rows, chunk), BF16),
            pltpu.VMEM((2, chunks, rows, chunk), BF16),
            pltpu.SemaphoreType.DMA((3,)),
            sems,
            sems,
            pltpu.SemaphoreType.DMA((2, chunks)),
            pltpu.SemaphoreType.DMA((2, chunks)),
        ],
        compiler_params=pltpu.CompilerParams(collective_id=2, has_side_effects=True, vmem_limit_bytes=VMEM_LIMIT),
        name="grads_reduce",
    )(g, ph, oh, wall)


def shards(n, n_mp, prompt_hidden, completion_hidden, queries, cotangent, kv_weight, prompt_of, comp_len):
    per, plen, model_dim = prompt_hidden.shape
    comps, slots, _ = completion_hidden.shape
    depth, _, kv_width = kv_weight.shape
    width = 2 * kv_width
    w = kv_weight.reshape(depth, width)
    ph = prompt_hidden.reshape(per * plen, model_dim)
    oh = completion_hidden.reshape(comps * slots, model_dim)
    attended, grad_queries, wall, g = layer(
        prompt_of, comp_len.reshape(-1), w, ph, oh, queries, cotangent, n, per
    )
    fp, fo, gw = grads(g, ph, oh, wall.reshape(model_dim, width), n, n_mp)
    return (
        attended,
        grad_queries,
        fp.reshape(per, plen, -1),
        fo.reshape(comps, slots, -1),
        gw.reshape(depth, 2, kv_width),
    )


def solution(mesh):
    in_specs = (
        P(("groups", "dp"), None, None),
        P(("groups", "dp"), None, None),
        P(("groups", "dp"), None, "mp"),
        P(("groups", "dp"), None, "mp"),
        P("dp", None, "mp"),
        P(("groups", "dp")),
        P(("groups", "dp"), None),
    )
    out_specs = (P(("groups", "dp"), None, "mp"),) * 5
    body = functools.partial(shards, mesh.shape["dp"], mesh.shape["mp"])
    return jax.shard_map(body, mesh=mesh, in_specs=in_specs, out_specs=out_specs, check_vma=False)
```
